128 devices in a mesh: grp: 16 (over z, y_lo, core), tp: 8 (over x, y_hi).
Axes of the slice: x: 4, y: 4 (y_hi: 2, y_lo: 2; y = y_hi * 2 + y_lo), z: 4, core: 2. Of those that a mesh axis runs over, the one named last changes fastest.
Arguments:
- hidden: bfloat16 [512, 16384], P(('grp', 'tp')), may hold values from -130 to 130
- gain: float32 [16384], replicated, may hold values from 0.5 to 1.5
- head: bfloat16 [16384, 65536], P(None, ('grp', 'tp')), may hold values from -3 to 3
Outputs:
- log_probs: float32 [512, 65536], P(('grp', 'tp'))
The draws below stay inside these ranges and needn't reach their ends.
All inputs are finite; a program needn't handle non-finite values.
Results may differ from the reference program's by a relative error of at most 0.00055.
Values may be sent and summed in bfloat16 or wider, within the bound.
A program may use at most 128 MiB of HBM per device.

```python
import math
import jax
import jax.numpy as jnp
from jax import lax

D = 16384
V_DEV = 512
TOK_DEV = 4
DEVICES = 128


def head_column(base, index):
    values = jax.random.normal(jax.random.fold_in(base, index), (D,), jnp.float32)
    return jnp.clip(values, -6.0, 6.0) * (3.0 / math.sqrt(D))


def draw_head(key, part):
    base = jax.random.fold_in(key, 11)
    columns = jax.vmap(lambda index: head_column(base, index))(jnp.arange(V_DEV * DEVICES))
    return columns.T.astype(jnp.bfloat16)


def draw_hidden(key, part):
    total_rows = TOK_DEV * DEVICES
    own_key = jax.random.fold_in(key, 23)
    row_scale = jnp.exp(jax.random.uniform(jax.random.fold_in(own_key, 1), (total_rows, 1), jnp.float32, 0.0, math.log(10.0)))
    col_scale = jnp.exp(jax.random.uniform(jax.random.fold_in(own_key, 2), (1, D), jnp.float32, 0.0, math.log(3.0)))
    rough = jnp.clip(jax.random.normal(jax.random.fold_in(own_key, 4), (total_rows, D), jnp.float32), -4.0, 4.0)
    values = rough * row_scale * col_scale
    return values.astype(jnp.bfloat16)


def setup_inputs(seed: int = 0) -> dict:
    splits = jax.random.split(jax.random.key(seed), 4)
    return {
        "hidden": draw_hidden(jax.random.fold_in(splits[3], 71), 0),
        "gain": jnp.clip(1.0 + 0.1 * jax.random.normal(splits[1], (D,), jnp.float32), 0.5, 1.5),
        "head": draw_head(jax.random.fold_in(splits[3], 71), 0),
    }


def reference(hidden, gain, head):
    values = hidden.astype(jnp.float32)
    mean_square = lax.optimization_barrier(jnp.mean(values * values, axis=-1, keepdims=True))
    normed = (values * lax.rsqrt(mean_square + 1e-05) * gain).astype(jnp.bfloat16)
    logits = jnp.dot(normed, head, preferred_element_type=jnp.float32)
    top = lax.optimization_barrier(jnp.max(logits, axis=-1, keepdims=True))
    total = lax.optimization_barrier(jnp.sum(jnp.exp(logits - top), axis=-1, keepdims=True))
    return logits - top - jnp.log(total)
```

```python
import jax
import jax.numpy as jnp
from jax import lax
from jax.experimental import pallas as pl
from jax.experimental.pallas import tpu as pltpu
from jax.sharding import PartitionSpec as P

MESH = pl.DeviceIdType.MESH
D, V, TOK = 16384, 512, 4
QUARTER = D // 4
TILE = 128
PARTS = ((0, 11, 6), (11, 22, 17), (22, 32, 27))
ORDERS = ((0, 1, 2), (1, 2, 0), (2, 0, 1))


def position():
    grp, tp = lax.axis_index("grp"), lax.axis_index("tp")
    return (tp // 2, (tp % 2) * 2 + (grp // 2) % 2, grp // 4), grp % 2


def device(at, core):
    x, y, z = at
    return ((z * 2 + y % 2) * 2 + core, x * 2 + y // 2)


def moved(at, axis, step):
    at = list(at)
    at[axis] = (at[axis] + step + 4) % 4
    return tuple(at)


def gather_matmul(hidden_ref, gain_ref, head_ref, out_ref, norm, piece, units, head, send, recv, local):
    me, core = position()
    partner = (me[0] + 1 - 2 * (me[0] % 2), me[1], me[2])
    member = (me[0] % 2) * 2 + core
    heads = []
    for quarter in range(4):
        copy = pltpu.make_async_copy(
            head_ref.at[pl.ds(quarter * QUARTER, QUARTER)], head.at[quarter], local.at[quarter]
        )
        copy.start()
        heads.append(copy)

    barrier = pltpu.get_barrier_semaphore()
    greeted = [device(moved(me, axis, step), core) for axis in range(3) for step in (1, -1)]
    greeted += [device(me, 1 - core), device(partner, 1 - core)]
    for other in greeted:
        pl.semaphore_signal(barrier, inc=1, device_id=other, device_id_type=MESH)

    values = hidden_ref[...].astype(jnp.float32)
    scale = lax.rsqrt(jnp.mean(values * values, axis=-1, keepdims=True) + 1e-05)
    for quarter in range(4):
        columns = slice(quarter * QUARTER, (quarter + 1) * QUARTER)
        normed = hidden_ref[:, columns].astype(jnp.float32) * scale * gain_ref[:, columns]
        wide = QUARTER // 4
        stacked = jnp.concatenate([normed[:, j * wide : (j + 1) * wide] for j in range(4)], axis=0)
        norm[quarter] = stacked.astype(jnp.bfloat16)
    pl.semaphore_wait(barrier, len(greeted))

    sent = []
    count = [0]

    def start(source, target, other):
        event = count[0]
        count[0] += 1
        copy = pltpu.make_async_remote_copy(
            source, target, send.at[event], recv.at[event], device_id=other, device_id_type=MESH
        )
        copy.start()
        sent.append(copy)
        return event

    swaps = []
    for relation in (1, 2, 3):
        i, c = member // 2, core
        i = 1 - i if relation & 2 else i
        c = 1 - c if relation & 1 else c
        other = device(partner if relation & 2 else me, c)
        event = start(norm.at[i * 2 + c], piece.at[member], other)
        swaps.append((event, i * 2 + c, other))
    mine = norm[member]
    piece[member] = mine
    for event, theirs, other in swaps:
        pltpu.make_async_remote_copy(
            norm.at[theirs], piece.at[theirs], send.at[event], recv.at[event], device_id=other, device_id_type=MESH
        ).wait_recv()
    wide = QUARTER // 4
    for j in range(4):
        rows = [piece[s].astype(jnp.float32)[j * 4 : j * 4 + 4] for s in range(4)]
        units[me[0], me[1], me[2], core, :, j * wide : (j + 1) * wide] = jnp.concatenate(rows, axis=0).astype(jnp.bfloat16)

    def view(part, at, of, span):
        order = ORDERS[part]
        index = [None] * 3
        for axis, value in zip(order, at):
            index[axis] = pl.ds(0, 4) if value is None else value
        first, last, middle = PARTS[part]
        low, high = {0: (first, middle), 1: (middle, last), 2: (first, last)}[span]
        return units.at[index[0], index[1], index[2], of, :, pl.ds(low * TILE, (high - low) * TILE)]

    sibling = device(me, 1 - core)

    def route(part):
        order = ORDERS[part]
        a, b, c = (me[axis] for axis in order)
        near = {(k, s): device(moved(me, order[k], s), core) for k in range(3) for s in (1, -1)}

        def at(da, db, dc):
            return (None if da is None else (a + da + 4) % 4, (b + db + 4) % 4, (c + dc + 4) % 4)

        def push(k, step, where, span=2):
            ref = view(part, at(*where), core, span)
            return start(ref, ref, near[k, step])

        def arrived(event, where, span=2, of=core, other=sibling):
            ref = view(part, at(*where), of, span)
            pltpu.make_async_remote_copy(
                ref, ref, send.at[event], recv.at[event], device_id=other, device_id_type=MESH
            ).wait_recv()

        across = {}

        def share(db, dc):
            ref = view(part, at(None, db, dc), core, 2)
            across[db, dc] = start(ref, ref, sibling)

        first = {s: push(0, s, (0, 0, 0)) for s in (1, -1)}
        line = {(0, s): push(1, s, (0, 0, 0)) for s in (1, -1)}
        yield
        second = {}
        for s, span in ((1, 0), (-1, 1)):
            arrived(first[s], (-s, 0, 0))
            second[s] = push(0, s, (-s, 0, 0), span)
            for t in (1, -1):
                line[-s, t] = push(1, t, (-s, 0, 0))
        yield
        for s, span in ((1, 0), (-1, 1)):
            arrived(second[s], (2, 0, 0), span)
        for t in (1, -1):
            line[2, t] = push(1, t, (2, 0, 0))
        plane = {(0, t): push(2, t, (None, 0, 0)) for t in (1, -1)}
        share(0, 0)
        yield
        onward = {}
        for da, t in ((0, 1), (0, -1), (-1, 1), (-1, -1), (1, 1), (1, -1), (2, 1), (2, -1)):
            arrived(line[da, t], (da, -t, 0))
            if (t == 1) == (da in (0, -1)):
                onward[da] = (push(1, t, (da, -t, 0)), t)
        for db in (-1, 1):
            for t in (1, -1):
                plane[db, t] = push(2, t, (None, db, 0))
            share(db, 0)
        yield
        for da in (0, -1, 1, 2):
            arrived(onward[da][0], (da, 2, 0))
        for t in (1, -1):
            plane[2, t] = push(2, t, (None, 2, 0))
        share(2, 0)
        yield
        last = {}
        for db in (0, -1, 1, 2):
            for t in (1, -1):
                arrived(plane[db, t], (None, db, -t))
                if (t == 1) == (db in (0, -1)):
                    last[db] = push(2, t, (None, db, -t))
                share(db, -t)
            yield
        for db in (0, 1, -1, 2):
            arrived(last[db], (None, db, 2))
            share(db, 2)
        yield
        yield lambda dc: [
            arrived(across[db, dc], (None, db, dc), of=1 - core) for db in (0, -1, 1, 2)
        ]

    def multiply(part, dc, first):
        axis = ORDERS[part][2]
        at = (me[axis] + dc + 4) % 4
        low, high, _ = PARTS[part]
        wide = (high - low) * TILE
        columns = pl.ds(low * TILE, wide)
        if axis == 0:
            for of in (0, 1):
                rows = units[at, :, :, of, :, columns].reshape(256, wide)
                weights = head[(at % 2) * 2 + of, columns]
                product = jnp.dot(rows, weights, preferred_element_type=jnp.float32).reshape(1, 4, 4, 16, V)
                out_ref[pl.ds(at // 2, 1)] += product
            return
        for i in (0, 1):
            for of in (0, 1):
                if axis == 1:
                    rows = jnp.concatenate([units[2 * h + i, at, :, of, :, columns].reshape(64, wide) for h in (0, 1)], axis=0)
                else:
                    rows = jnp.concatenate([units[2 * h + i, :, at, of, :, columns].reshape(64, wide) for h in (0, 1)], axis=0)
                weights = head[i * 2 + of, columns]
                product = jnp.dot(rows, weights, preferred_element_type=jnp.float32).reshape(2, 4, 16, V)
                if axis == 1:
                    out_ref[:, at] += product
                else:
                    out_ref[:, :, at] += product

    routes = [route(part) for part in range(3)]
    for _ in range(5):
        for r in routes:
            next(r)
    out_ref[...] = jnp.zeros_like(out_ref)
    for _ in range(4):
        for r in routes:
            next(r)
    for r in routes:
        next(r)
    fetched = [next(r) for r in routes]
    for copy in heads:
        copy.wait()
    for part in range(3):
        for dc in (0, -1, 1, 2):
            fetched[part](dc)
            multiply(part, dc, False)
    for copy in sent:
        copy.wait_send()


EVENTS = 3 + 3 * 44


def on_device(hidden, gain, head):
    logits = pl.pallas_call(
        gather_matmul,
        out_shape=jax.ShapeDtypeStruct((2, 4, 4, 16, V), jnp.float32),
        in_specs=[
            pl.BlockSpec(memory_space=pltpu.VMEM),
            pl.BlockSpec(memory_space=pltpu.VMEM),
            pl.BlockSpec(memory_space=pl.ANY),
        ],
        out_specs=pl.BlockSpec(memory_space=pltpu.VMEM),
        scratch_shapes=[
            pltpu.VMEM((4, 16, QUARTER // 4), jnp.bfloat16),
            pltpu.VMEM((4, 16, QUARTER // 4), jnp.bfloat16),
            pltpu.VMEM((4, 4, 4, 2, 16, QUARTER), jnp.bfloat16),
            pltpu.VMEM((4, QUARTER, V), jnp.bfloat16),
            pltpu.SemaphoreType.DMA((EVENTS,)),
            pltpu.SemaphoreType.DMA((EVENTS,)),
            pltpu.SemaphoreType.DMA((4,)),
        ],
        compiler_params=pltpu.CompilerParams(
            collective_id=0, has_side_effects=True, vmem_limit_bytes=56 * 2**20
        ),
        cost_estimate=pl.CostEstimate(
            flops=2 * 512 * D * V, bytes_accessed=D * V * 2, transcendentals=0
        ),
    )(hidden, gain.reshape(1, D), head)
    pieces = logits.reshape(2, 2, 2, 4, 2, 2, TOK, V).transpose(3, 2, 5, 0, 4, 1, 6, 7)
    pieces = pieces.reshape(128, TOK, V)
    owned = lax.all_to_all(pieces, ("grp", "tp"), split_axis=0, concat_axis=0, tiled=True)
    owned = owned.transpose(1, 0, 2).reshape(TOK, 128 * V)
    top = jnp.max(owned, axis=-1, keepdims=True)
    total = jnp.sum(jnp.exp(owned - top), axis=-1, keepdims=True)
    return owned - top - jnp.log(total)


def solution(mesh):
    return jax.shard_map(
        on_device,
        mesh=mesh,
        in_specs=(P(("grp", "tp"), None), P(), P(None, ("grp", "tp"))),
        out_specs=P(("grp", "tp"), None),
        check_vma=False,
    )
```

```python
import jax
import jax.numpy as jnp
from jax import lax
from jax.experimental import pallas as pl
from jax.experimental.pallas import tpu as pltpu
from jax.sharding import PartitionSpec as P

MESH = pl.DeviceIdType.MESH
D, V, TOK = 16384, 512, 4
QUARTER = D // 4
TILE = 128
PARTS = ((0, 11, 6), (11, 22, 17), (22, 32, 27))
STEEP, FLOOR, LOWEST = 17.5, 8.0, 125.0
ORDERS = ((0, 1, 2), (1, 2, 0), (2, 0, 1))


def position():
    grp, tp = lax.axis_index("grp"), lax.axis_index("tp")
    return (tp // 2, (tp % 2) * 2 + (grp // 2) % 2, grp // 4), grp % 2


def device(at, core):
    x, y, z = at
    return ((z * 2 + y % 2) * 2 + core, x * 2 + y // 2)


def moved(at, axis, step):
    at = list(at)
    at[axis] = (at[axis] + step + 4) % 4
    return tuple(at)


def encode(d):
    size = jnp.exp2(STEEP * jnp.log2(1.0 + jnp.abs(d) * (1.0 / FLOOR)) - LOWEST)
    return jnp.where(d < 0, -size, size).astype(jnp.bfloat16).astype(jnp.float32)


def decode(v):
    size = FLOOR * (jnp.exp2((jnp.log2(jnp.abs(v)) + LOWEST) * (1.0 / STEEP)) - 1.0)
    return jnp.where(v < 0, -size, size)


def gather_matmul(
    hidden_ref, gain_ref, head_ref, out_ref, norm, piece, units, head, acc, codes, got, logits, send, recv, local, spread
):
    me, core = position()
    partner = (me[0] + 1 - 2 * (me[0] % 2), me[1], me[2])
    member = (me[0] % 2) * 2 + core
    heads = []
    for quarter in range(4):
        copy = pltpu.make_async_copy(
            head_ref.at[pl.ds(quarter * QUARTER, QUARTER)], head.at[quarter], local.at[quarter]
        )
        copy.start()
        heads.append(copy)

    barrier = pltpu.get_barrier_semaphore()
    greeted = [device(moved(me, axis, step), core) for axis in range(3) for step in (1, -1)]
    greeted += [device(me, 1 - core), device(partner, 1 - core)]
    for other in greeted:
        pl.semaphore_signal(barrier, inc=1, device_id=other, device_id_type=MESH)

    values = hidden_ref[...].astype(jnp.float32)
    scale = lax.rsqrt(jnp.mean(values * values, axis=-1, keepdims=True) + 1e-05)
    for quarter in range(4):
        columns = slice(quarter * QUARTER, (quarter + 1) * QUARTER)
        normed = hidden_ref[:, columns].astype(jnp.float32) * scale * gain_ref[:, columns]
        wide = QUARTER // 4
        stacked = jnp.concatenate([normed[:, j * wide : (j + 1) * wide] for j in range(4)], axis=0)
        norm[quarter] = stacked.astype(jnp.bfloat16)
    pl.semaphore_wait(barrier, len(greeted))

    sent = []
    count = [0]

    def start(source, target, other):
        event = count[0]
        count[0] += 1
        copy = pltpu.make_async_remote_copy(
            source, target, send.at[event], recv.at[event], device_id=other, device_id_type=MESH
        )
        copy.start()
        sent.append(copy)
        return event

    swaps = []
    for relation in (1, 2, 3):
        i, c = member // 2, core
        i = 1 - i if relation & 2 else i
        c = 1 - c if relation & 1 else c
        other = device(partner if relation & 2 else me, c)
        event = start(norm.at[i * 2 + c], piece.at[member], other)
        swaps.append((event, i * 2 + c, other))
    mine = norm[member]
    piece[member] = mine
    for event, theirs, other in swaps:
        pltpu.make_async_remote_copy(
            norm.at[theirs], piece.at[theirs], send.at[event], recv.at[event], device_id=other, device_id_type=MESH
        ).wait_recv()
    wide = QUARTER // 4
    for j in range(4):
        rows = [piece[s].astype(jnp.float32)[j * 4 : j * 4 + 4] for s in range(4)]
        units[me[0], me[1], me[2], core, :, j * wide : (j + 1) * wide] = jnp.concatenate(rows, axis=0).astype(jnp.bfloat16)

    def view(part, at, of, span):
        order = ORDERS[part]
        index = [None] * 3
        for axis, value in zip(order, at):
            index[axis] = pl.ds(0, 4) if value is None else value
        first, last, middle = PARTS[part]
        low, high = {0: (first, middle), 1: (middle, last), 2: (first, last)}[span]
        return units.at[index[0], index[1], index[2], of, :, pl.ds(low * TILE, (high - low) * TILE)]

    sibling = device(me, 1 - core)
    arrivals = {}

    def route(part):
        order = ORDERS[part]
        a, b, c = (me[axis] for axis in order)
        near = {(k, s): device(moved(me, order[k], s), core) for k in range(3) for s in (1, -1)}

        def at(da, db, dc):
            return (None if da is None else (a + da + 4) % 4, (b + db + 4) % 4, (c + dc + 4) % 4)

        def push(k, step, where, span=2):
            ref = view(part, at(*where), core, span)
            return start(ref, ref, near[k, step])

        def arrived(event, where, span=2, of=core, other=sibling):
            ref = view(part, at(*where), of, span)
            pltpu.make_async_remote_copy(
                ref, ref, send.at[event], recv.at[event], device_id=other, device_id_type=MESH
            ).wait_recv()

        across = {}

        def share(db, dc):
            ref = view(part, at(None, db, dc), core, 2)
            across[db, dc] = start(ref, ref, sibling)

        arrivals[part] = lambda db, dc: arrived(across[db, dc], (None, db, dc), of=1 - core)

        first = {s: push(0, s, (0, 0, 0)) for s in (1, -1)}
        line = {(0, s): push(1, s, (0, 0, 0)) for s in (1, -1)}
        yield
        second = {}
        for s, span in ((1, 0), (-1, 1)):
            arrived(first[s], (-s, 0, 0))
            second[s] = push(0, s, (-s, 0, 0), span)
            for t in (1, -1):
                line[-s, t] = push(1, t, (-s, 0, 0))
        yield
        for s, span in ((1, 0), (-1, 1)):
            arrived(second[s], (2, 0, 0), span)
        for t in (1, -1):
            line[2, t] = push(1, t, (2, 0, 0))
        plane = {(0, t): push(2, t, (None, 0, 0)) for t in (1, -1)}
        share(0, 0)
        yield
        onward = {}
        for da, t in ((0, 1), (0, -1), (-1, 1), (-1, -1), (1, 1), (1, -1), (2, 1), (2, -1)):
            arrived(line[da, t], (da, -t, 0))
            if (t == 1) == (da in (0, -1)):
                onward[da] = (push(1, t, (da, -t, 0)), t)
        for db in (-1, 1):
            for t in (1, -1):
                plane[db, t] = push(2, t, (None, db, 0))
            share(db, 0)
        yield
        for da in (0, -1, 1, 2):
            arrived(onward[da][0], (da, 2, 0))
        for t in (1, -1):
            plane[2, t] = push(2, t, (None, 2, 0))
        share(2, 0)
        yield
        last = {}
        for db in (0, -1, 1, 2):
            for t in (1, -1):
                arrived(plane[db, t], (None, db, -t))
                if (t == 1) == (db in (0, -1)):
                    last[db] = push(2, t, (None, db, -t))
                share(db, -t)
            yield
        for db in (0, 1, -1, 2):
            arrived(last[db], (None, db, 2))
            share(db, 2)
            yield

    def multiply(part, dc):
        axis = ORDERS[part][2]
        at = (me[axis] + dc + 4) % 4
        low, high, _ = PARTS[part]
        wide = (high - low) * TILE
        columns = pl.ds(low * TILE, wide)
        if axis == 0:
            for of in (0, 1):
                rows = units[at, :, :, of, :, columns].reshape(256, wide)
                weights = head[(at % 2) * 2 + of, columns]
                product = jnp.dot(rows, weights, preferred_element_type=jnp.float32).reshape(1, 4, 4, 16, V)
                acc[pl.ds(at // 2, 1)] += product
            return
        for i in (0, 1):
            for of in (0, 1):
                if axis == 1:
                    rows = jnp.concatenate([units[2 * h + i, at, :, of, :, columns].reshape(64, wide) for h in (0, 1)], axis=0)
                else:
                    rows = jnp.concatenate([units[2 * h + i, :, at, of, :, columns].reshape(64, wide) for h in (0, 1)], axis=0)
                weights = head[i * 2 + of, columns]
                product = jnp.dot(rows, weights, preferred_element_type=jnp.float32).reshape(2, 4, 16, V)
                if axis == 1:
                    acc[:, at] += product
                else:
                    acc[:, :, at] += product

    routes = [route(part) for part in range(3)]

    def advance(steps=1):
        for _ in range(steps):
            for r in routes:
                next(r)

    advance(4)
    acc[...] = jnp.zeros_like(acc)
    for copy in heads:
        copy.wait()
    advance(2)

    def sibling_plane(part, dc):
        for db in (0, -1, 1, 2):
            arrivals[part](db, dc)

    for step in range(3):
        sibling_plane(step, 0)
        multiply(step, 0)
        advance(1)
    for part in range(3):
        for dc in (-1, 1):
            sibling_plane(part, dc)
            multiply(part, dc)
    advance(4)
    for part in range(3):
        sibling_plane(part, 2)
        multiply(part, 2)

    grp, tp = lax.axis_index("grp"), lax.axis_index("tp")
    here = grp * 8 + tp

    def messages(xh, y, z):
        rows = acc[xh, y, z]
        anchor = decode(encode(rows[:, :1]))
        lane = lax.broadcasted_iota(jnp.int32, rows.shape, 1)
        coded = encode(jnp.where(lane == 0, rows, rows - anchor))
        for m in range(4):
            yield m, jnp.concatenate(
                [coded[4 * m : 4 * m + 4, TILE * j : TILE * (j + 1)] for j in range(4)], axis=0
            ).astype(jnp.bfloat16)

    def deliver(slot, i, c, xh, y, z):
        pltpu.make_async_remote_copy(
            codes.at[slot], got.at[here], spread.at[0], spread.at[1],
            device_id=device((2 * xh + i, y, z), c), device_id_type=MESH,
        ).start()

    def emit(k, _):
        xh, y, z = (me[0] // 2 + k) % 2, (me[1] + k // 2) % 4, (me[2] + k // 8) % 4
        for m, message in messages(xh, y, z):
            codes[k * 4 + m] = message
            deliver(k * 4 + m, m // 2, m % 2, xh, y, z)
        return 0

    lax.fori_loop(1, 32, emit, 0)
    xh = me[0] // 2
    for m, message in messages(xh, me[1], me[2]):
        codes[m] = message
    got[here] = codes[member]
    for relation in (1, 2, 3):
        i = 1 - member // 2 if relation & 2 else member // 2
        c = 1 - core if relation & 1 else core
        deliver(i * 2 + c, i, c, xh, me[1], me[2])
    pltpu.make_async_remote_copy(
        codes.at[pl.ds(0, 127)], got.at[pl.ds(0, 127)], spread.at[0], spread.at[1],
        device_id=sibling, device_id_type=MESH,
    ).wait()
    for copy in sent:
        copy.wait_send()

    def four(rows):
        return jnp.concatenate([rows] * 4, axis=0)

    first_lane = lax.broadcasted_iota(jnp.int32, (16, TILE), 1) == 0
    first = first_lane & (lax.broadcasted_iota(jnp.int32, (16, TILE), 0) < 4)

    def open_message(s, top):
        d = decode(got[s].astype(jnp.float32))
        anchor = four(d[:4, :1])
        values = jnp.where(first, d, d + anchor)
        logits[s] = values
        return jnp.maximum(top, values)

    def by_token(rows, combine, reduce):
        each = reduce(rows, axis=1, keepdims=True)
        return combine(combine(each[:4], each[4:8]), combine(each[8:12], each[12:]))

    top = lax.fori_loop(0, 128, open_message, jnp.full((16, TILE), -jnp.inf, jnp.float32), unroll=4)
    top = by_token(top, jnp.maximum, jnp.max)
    top_rows = jnp.broadcast_to(four(top), (16, TILE))
    total = lax.fori_loop(
        0, 128, lambda s, t: t + jnp.exp(logits[s] - top_rows), jnp.zeros((16, TILE), jnp.float32), unroll=8
    )
    total = by_token(total, jnp.add, jnp.sum)
    top_row = jnp.broadcast_to(top, (4, TILE))
    log_row = jnp.broadcast_to(jnp.log(total), (4, TILE))

    def finish(s, _):
        for j in range(4):
            out_ref[s, :, TILE * j : TILE * (j + 1)] = logits[s, 4 * j : 4 * j + 4] - top_row - log_row
        return 0

    lax.fori_loop(0, 128, finish, 0, unroll=8)


EVENTS = 3 + 3 * 44


def on_device(hidden, gain, head):
    log_probs = pl.pallas_call(
        gather_matmul,
        out_shape=jax.ShapeDtypeStruct((128, TOK, V), jnp.float32),
        in_specs=[
            pl.BlockSpec(memory_space=pltpu.VMEM),
            pl.BlockSpec(memory_space=pltpu.VMEM),
            pl.BlockSpec(memory_space=pl.ANY),
        ],
        out_specs=pl.BlockSpec(memory_space=pltpu.VMEM),
        scratch_shapes=[
            pltpu.VMEM((4, 16, QUARTER // 4), jnp.bfloat16),
            pltpu.VMEM((4, 16, QUARTER // 4), jnp.bfloat16),
            pltpu.VMEM((4, 4, 4, 2, 16, QUARTER), jnp.bfloat16),
            pltpu.VMEM((4, QUARTER, V), jnp.bfloat16),
            pltpu.VMEM((2, 4, 4, 16, V), jnp.float32),
            pltpu.VMEM((128, 16, TILE), jnp.bfloat16),
            pltpu.VMEM((128, 16, TILE), jnp.bfloat16),
            pltpu.VMEM((128, 16, TILE), jnp.float32),
            pltpu.SemaphoreType.DMA((EVENTS,)),
            pltpu.SemaphoreType.DMA((EVENTS,)),
            pltpu.SemaphoreType.DMA((4,)),
            pltpu.SemaphoreType.DMA((2,)),
        ],
        compiler_params=pltpu.CompilerParams(
            collective_id=0, has_side_effects=True, vmem_limit_bytes=56 * 2**20
        ),
        cost_estimate=pl.CostEstimate(
            flops=2 * 512 * D * V, bytes_accessed=D * V * 2, transcendentals=0
        ),
    )(hidden, gain.reshape(1, D), head)
    return log_probs.transpose(1, 0, 2).reshape(TOK, 128 * V)


def solution(mesh):
    return jax.shard_map(
        on_device,
        mesh=mesh,
        in_specs=(P(("grp", "tp"), None), P(), P(None, ("grp", "tp"))),
        out_specs=P(("grp", "tp"), None),
        check_vma=False,
    )
```

```python
import jax
import jax.numpy as jnp
from jax import lax
from jax.experimental import pallas as pl
from jax.experimental.pallas import tpu as pltpu
from jax.sharding import PartitionSpec as P

MESH = pl.DeviceIdType.MESH
D, V, TOK = 16384, 512, 4
QUARTER = D // 4
TILE = 128
PARTS = ((0, 11, 6), (11, 22, 17), (22, 32, 27))
ORDERS = ((0, 1, 2), (1, 2, 0), (2, 0, 1))
STEEP, FLOOR, LOWEST = 17.5, 8.0, 125.0
EVENTS = 1 + 3 * 39


def position():
    grp, tp = lax.axis_index("grp"), lax.axis_index("tp")
    return (tp // 2, (tp % 2) * 2 + (grp // 2) % 2, grp // 4), grp % 2


def device(at, core):
    x, y, z = at
    return ((z * 2 + y % 2) * 2 + core, x * 2 + y // 2)


def moved(at, axis, step):
    at = list(at)
    at[axis] = (at[axis] + step + 4) % 4
    return tuple(at)


def encode(d):
    size = jnp.exp2(STEEP * jnp.log2(1.0 + jnp.abs(d) * (1.0 / FLOOR)) - LOWEST)
    return jnp.where(d < 0, -size, size).astype(jnp.bfloat16).astype(jnp.float32)


def decode(v):
    size = FLOOR * (jnp.exp2((jnp.log2(jnp.abs(v)) + LOWEST) * (1.0 / STEEP)) - 1.0)
    return jnp.where(v < 0, -size, size)


def kernel(
    hidden_ref, gain_ref, head_ref, out_ref, norm, piece, units, head, acc, codes, got, logits, send, recv, local, spread
):
    me, core = position()
    sibling = device(me, 1 - core)
    heads = []
    for quarter in range(4):
        copy = pltpu.make_async_copy(
            head_ref.at[pl.ds(quarter * QUARTER, QUARTER)], head.at[quarter], local.at[quarter]
        )
        copy.start()
        heads.append(copy)

    barrier = pltpu.get_barrier_semaphore()
    greeted = [device(moved(me, axis, step), core) for axis in range(3) for step in (1, -1, 2)]
    greeted.append(sibling)
    for other in greeted:
        pl.semaphore_signal(barrier, inc=1, device_id=other, device_id_type=MESH)

    values = hidden_ref[...].astype(jnp.float32)
    scale = lax.rsqrt(jnp.mean(values * values, axis=-1, keepdims=True) + 1e-05)
    wide = D // 8
    for half in range(2):
        rows = []
        for j in range(4):
            columns = slice(half * 2 * QUARTER + j * wide, half * 2 * QUARTER + (j + 1) * wide)
            rows.append(hidden_ref[:, columns].astype(jnp.float32) * scale * gain_ref[:, columns])
        norm[half] = jnp.concatenate(rows, axis=0).astype(jnp.bfloat16)
    pl.semaphore_wait(barrier, len(greeted))

    sent = {}
    count = [0]

    def start(source, target, other):
        event = count[0]
        count[0] += 1
        copy = pltpu.make_async_remote_copy(
            source, target, send.at[event], recv.at[event], device_id=other, device_id_type=MESH
        )
        copy.start()
        sent[event] = copy
        return event

    event = start(norm.at[1 - core], piece.at[core], sibling)
    piece[core] = norm[core]
    pltpu.make_async_remote_copy(
        norm.at[core], piece.at[1 - core], send.at[event], recv.at[event], device_id=sibling, device_id_type=MESH
    ).wait_recv()
    both = [piece[s].astype(jnp.float32) for s in (0, 1)]
    for j in (0, 1):
        rows = [both[s][8 * h + 4 * j : 8 * h + 4 * j + 4] for h in (0, 1) for s in (0, 1)]
        units[me[0], me[1], me[2], core, :, j * wide : (j + 1) * wide] = jnp.concatenate(rows, axis=0).astype(jnp.bfloat16)

    def view(part, at, of, span):
        order = ORDERS[part]
        index = [None] * 3
        for axis, value in zip(order, at):
            index[axis] = pl.ds(0, 4) if value is None else value
        first, last, middle = PARTS[part]
        low, high = {0: (first, middle), 1: (middle, last), 2: (first, last)}[span]
        return units.at[index[0], index[1], index[2], of, :, pl.ds(low * TILE, (high - low) * TILE)]

    class Route:
        def __init__(self, part):
            self.part = part
            order = ORDERS[part]
            self.at = [me[axis] for axis in order]
            self.near = {(k, s): device(moved(me, order[k], s), core) for k in range(3) for s in (1, -1, 2)}
            self.events = {}

        def where(self, da, db, dc):
            a, b, c = self.at
            return (None if da is None else (a + da + 4) % 4, (b + db + 4) % 4, (c + dc + 4) % 4)

        def push(self, name, k, step, where, span=2):
            ref = view(self.part, self.where(*where), core, span)
            self.events[name] = start(ref, ref, self.near[k, step])

        def share(self, db, dc):
            ref = view(self.part, self.where(None, db, dc), core, 2)
            self.events["share", db, dc] = start(ref, ref, sibling)

        def arrived(self, name, where, span=2, of=core):
            ref = view(self.part, self.where(*where), of, span)
            event = self.events[name]
            pltpu.make_async_remote_copy(
                ref, ref, send.at[event], recv.at[event], device_id=sibling, device_id_type=MESH
            ).wait_recv()

    routes = [Route(part) for part in range(3)]
    for r in routes:
        for s in (1, -1, 2):
            r.push(("a", s), 0, s, (0, 0, 0))
    acc[...] = jnp.zeros_like(acc)
    for r in routes:
        for s in (1, -1, 2):
            r.arrived(("a", s), (-s, 0, 0))
        for s in (1, -1):
            r.push(("b", s), 1, s, (None, 0, 0))
    for r in routes:
        r.share(0, 0)
    for r in routes:
        for s in (1, -1):
            r.push(("c", 0, s), 2, s, (None, 0, 0))
    for r in routes:
        for s, span in ((1, 0), (-1, 1)):
            r.arrived(("b", s), (None, -s, 0))
            r.push(("bb", s), 1, s, (None, -s, 0), span)
    for db in (-1, 1):
        for r in routes:
            for s in (1, -1):
                r.push(("c", db, s), 2, s, (None, db, 0))
            r.share(db, 0)
    for r in routes:
        for s, span in ((1, 0), (-1, 1)):
            r.arrived(("bb", s), (None, 2, 0), span)
        for s in (1, -1):
            r.push(("c", 2, s), 2, s, (None, 2, 0))
        r.share(2, 0)

    def onward(db):
        for r in routes:
            for s, span in ((1, 0), (-1, 1)):
                r.arrived(("c", db, s), (None, db, -s))
                r.push(("cc", db, s), 2, s, (None, db, -s), span)
            for s in (1, -1):
                r.share(db, -s)

    def last(db):
        for r in routes:
            for s, span in ((1, 0), (-1, 1)):
                r.arrived(("cc", db, s), (None, db, 2), span)
            r.share(db, 2)

    def multiply(part, *planes):
        r = routes[part]
        axis = ORDERS[part][2]
        at = [r.where(0, 0, dc)[2] for dc in planes]
        for dc in planes:
            for db in (0, -1, 1, 2):
                r.arrived(("share", db, dc), (None, db, dc), of=1 - core)
        low, high, _ = PARTS[part]
        columns = pl.ds(low * TILE, (high - low) * TILE)
        for of in (0, 1):
            for h in (0, 1):
                rows = []
                for p in at:
                    index = [slice(None)] * 3
                    index[axis] = p
                    rows.append(units[(*index, of, slice(8 * h, 8 * h + 8), columns)].reshape(128, (high - low) * TILE))
                product = jnp.dot(
                    jnp.concatenate(rows, axis=0) if len(rows) > 1 else rows[0],
                    head[of * 2 + h, columns],
                    preferred_element_type=jnp.float32,
                )
                for n, p in enumerate(at):
                    index = [slice(None)] * 3
                    index[axis] = p
                    acc[tuple(index)] += product[n * 128 : (n + 1) * 128].reshape(4, 4, 8, V)

    grp, tp = lax.axis_index("grp"), lax.axis_index("tp")
    here = grp * 8 + tp

    def deliver(slot, s, at):
        pltpu.make_async_remote_copy(
            codes.at[slot, s], got.at[here], spread.at[0], spread.at[1], device_id=device(at, s), device_id_type=MESH
        ).start()

    def chip(dx, dy, dz):
        return tuple(lax.rem(axis + d, 4) for axis, d in zip(me, (dx, dy, dz)))

    def code(rows, slots):
        anchor = decode(encode(rows[:, :, :1]))
        lane = lax.broadcasted_iota(jnp.int32, rows.shape, 2)
        coded = encode(jnp.where(lane == 0, rows, rows - anchor))
        for s in range(2):
            tiles = [coded[:, 4 * s : 4 * s + 4, TILE * j : TILE * (j + 1)] for j in range(4)]
            message = jnp.concatenate(tiles, axis=1).astype(jnp.bfloat16)
            for n, slot in enumerate(slots):
                codes[slot, s] = message[n]

    def place(at):
        return (at[0] * 4 + at[1]) * 4 + at[2]

    def code_some(chips):
        code(jnp.stack([acc[at] for at in chips]), [place(at) for at in chips])

    def emit(at):
        for s in range(2):
            deliver(place(at), s, at)

    def close(k):
        return lax.rem(k + 3, 4)

    for copy in heads:
        copy.wait()
    onward(0)
    multiply(0, 0)
    onward(-1)
    multiply(1, 0)
    onward(1)
    multiply(2, 0)
    onward(2)
    multiply(0, -1, 1)
    last(0)
    multiply(1, -1, 1)
    last(-1)
    multiply(2, -1, 1)
    last(1)

    def near(k, _):
        for dx in (3, 0, 1):
            code_some([chip(dx, close(k), dz) for dz in (3, 0, 1)])
        for dx in (3, 0, 1):
            for dz in (3, 0, 1):
                if (dx, dz) != (0, 0):
                    emit(chip(dx, close(k), dz))
        return 0

    lax.fori_loop(0, 3, near, 0)
    emit(chip(0, 3, 0))
    emit(chip(0, 1, 0))
    own = place(me)
    deliver(own, 1 - core, me)
    got[here] = codes[own, core]

    last(2)
    for part in range(3):
        multiply(part, 2)

    def far(k, _):
        code_some([chip(2, dy, k) for dy in range(4)])
        for dy in range(4):
            emit(chip(2, dy, k))
        return 0

    def rest(k, _):
        code_some([chip(close(k), 2, dz) for dz in range(4)] + [chip(close(k), dy, 2) for dy in (3, 0, 1)])
        for dz in range(4):
            emit(chip(close(k), 2, dz))
        for dy in (3, 0, 1):
            emit(chip(close(k), dy, 2))
        return 0

    lax.fori_loop(0, 3, rest, 0)
    lax.fori_loop(0, 4, far, 0)
    for copy in sent.values():
        copy.wait_send()
    pltpu.make_async_remote_copy(
        got.at[pl.ds(0, 127)], got.at[pl.ds(0, 127)], spread.at[0], spread.at[1],
        device_id=sibling, device_id_type=MESH,
    ).wait()

    def four(rows):
        return jnp.concatenate([rows] * 4, axis=rows.ndim - 2)

    some = 16
    first = lax.broadcasted_iota(jnp.int32, (some, 16, TILE), 2) == 0
    first = first & (lax.broadcasted_iota(jnp.int32, (some, 16, TILE), 1) < 4)

    def open_messages(n, top):
        at = pl.ds(n * some, some)
        d = decode(got[at].astype(jnp.float32))
        values = jnp.where(first, d, d + four(d[:, :4, :1]))
        logits[at] = values
        return jnp.maximum(top, jnp.max(values, axis=0))

    def by_token(rows, combine, reduce):
        each = reduce(rows, axis=1, keepdims=True)
        return combine(combine(each[:4], each[4:8]), combine(each[8:12], each[12:]))

    top = lax.fori_loop(0, 128 // some, open_messages, jnp.full((16, TILE), -jnp.inf, jnp.float32))
    top = by_token(top, jnp.maximum, jnp.max)
    top_rows = jnp.broadcast_to(four(top), (16, TILE))

    def add(n, total):
        return total + jnp.sum(jnp.exp(logits[pl.ds(n * some, some)] - top_rows), axis=0)

    total = lax.fori_loop(0, 128 // some, add, jnp.zeros((16, TILE), jnp.float32))
    total = by_token(total, jnp.add, jnp.sum)
    top_row = jnp.broadcast_to(top, (TOK, TILE))
    log_row = jnp.broadcast_to(jnp.log(total), (TOK, TILE))

    def finish(n, _):
        at = pl.ds(n * some, some)
        for j in range(4):
            out_ref[at, :, TILE * j : TILE * (j + 1)] = logits[at, 4 * j : 4 * j + 4] - top_row - log_row
        return 0

    lax.fori_loop(0, 128 // some, finish, 0)


def on_device(hidden, gain, head):
    log_probs = pl.pallas_call(
        kernel,
        out_shape=jax.ShapeDtypeStruct((128, TOK, V), jnp.float32),
        in_specs=[
            pl.BlockSpec(memory_space=pltpu.VMEM),
            pl.BlockSpec(memory_space=pltpu.VMEM),
            pl.BlockSpec(memory_space=pl.ANY),
        ],
        out_specs=pl.BlockSpec(memory_space=pltpu.VMEM),
        scratch_shapes=[
            pltpu.VMEM((2, 16, D // 8), jnp.bfloat16),
            pltpu.VMEM((2, 16, D // 8), jnp.bfloat16),
            pltpu.VMEM((4, 4, 4, 2, 16, QUARTER), jnp.bfloat16),
            pltpu.VMEM((4, QUARTER, V), jnp.bfloat16),
            pltpu.VMEM((4, 4, 4, 8, V), jnp.float32),
            pltpu.VMEM((64, 2, 16, TILE), jnp.bfloat16),
            pltpu.VMEM((128, 16, TILE), jnp.bfloat16),
            pltpu.VMEM((128, 16, TILE), jnp.float32),
            pltpu.SemaphoreType.DMA((EVENTS,)),
            pltpu.SemaphoreType.DMA((EVENTS,)),
            pltpu.SemaphoreType.DMA((4,)),
            pltpu.SemaphoreType.DMA((2,)),
        ],
        compiler_params=pltpu.CompilerParams(
            collective_id=0, has_side_effects=True, vmem_limit_bytes=50 * 2**20
        ),
        cost_estimate=pl.CostEstimate(
            flops=2 * 512 * D * V, bytes_accessed=D * V * 2, transcendentals=0
        ),
    )(hidden, gain.reshape(1, D), head)
    return log_probs.transpose(1, 0, 2).reshape(TOK, 128 * V)


def solution(mesh):
    return jax.shard_map(
        on_device,
        mesh=mesh,
        in_specs=(P(("grp", "tp"), None), P(), P(None, ("grp", "tp"))),
        out_specs=P(("grp", "tp"), None),
        check_vma=False,
    )
```

```python
import jax
import jax.numpy as jnp
from jax import lax
from jax.experimental import pallas as pl
from jax.experimental.pallas import tpu as pltpu
from jax.sharding import PartitionSpec as P

MESH = pl.DeviceIdType.MESH
D, V, TOK = 16384, 512, 4
QUARTER = D // 4
TILE = 128
PARTS = ((0, 11, 6), (11, 22, 17), (22, 32, 27))
ORDERS = ((0, 1, 2), (1, 2, 0), (2, 0, 1))
STEEP, FLOOR, LOWEST = 17.5, 8.0, 125.0
EVENTS = 1 + 3 * 51


def position():
    grp, tp = lax.axis_index("grp"), lax.axis_index("tp")
    return (tp // 2, (tp % 2) * 2 + (grp // 2) % 2, grp // 4), grp % 2


def device(at, core):
    x, y, z = at
    return ((z * 2 + y % 2) * 2 + core, x * 2 + y // 2)


def moved(at, axis, step):
    at = list(at)
    at[axis] = (at[axis] + step + 4) % 4
    return tuple(at)


def encode(d):
    size = jnp.exp2(STEEP * jnp.log2(1.0 + jnp.abs(d) * (1.0 / FLOOR)) - LOWEST)
    return jnp.where(d < 0, -size, size).astype(jnp.bfloat16).astype(jnp.float32)


def decode(v):
    size = FLOOR * (jnp.exp2((jnp.log2(jnp.abs(v)) + LOWEST) * (1.0 / STEEP)) - 1.0)
    return jnp.where(v < 0, -size, size)


def kernel(
    hidden_hbm, gain_hbm, head_ref, out_ref, hidden_ref, gain_ref, norm, piece, units, head, acc, codes, got, logits, send, recv, local, spread
):
    me, core = position()
    sibling = device(me, 1 - core)
    inputs = [
        pltpu.make_async_copy(hidden_hbm, hidden_ref, local.at[4]),
        pltpu.make_async_copy(gain_hbm, gain_ref, local.at[5]),
    ]
    for copy in inputs:
        copy.start()
    heads = []
    for quarter in range(4):
        copy = pltpu.make_async_copy(
            head_ref.at[pl.ds(quarter * QUARTER, QUARTER)], head.at[quarter], local.at[quarter]
        )
        copy.start()
        heads.append(copy)

    barrier = pltpu.get_barrier_semaphore()
    greeted = [device(moved(me, axis, step), core) for axis in range(3) for step in (1, -1, 2)]
    greeted.append(sibling)
    for other in greeted:
        pl.semaphore_signal(barrier, inc=1, device_id=other, device_id_type=MESH)

    for copy in inputs:
        copy.wait()
    values = hidden_ref[...].astype(jnp.float32)
    scale = lax.rsqrt(jnp.mean(values * values, axis=-1, keepdims=True) + 1e-05)
    wide = D // 8
    for half in range(2):
        rows = []
        for j in range(4):
            columns = slice(half * 2 * QUARTER + j * wide, half * 2 * QUARTER + (j + 1) * wide)
            rows.append(hidden_ref[:, columns].astype(jnp.float32) * scale * gain_ref[:, columns])
        norm[half] = jnp.concatenate(rows, axis=0).astype(jnp.bfloat16)
    pl.semaphore_wait(barrier, len(greeted))

    sent = {}
    count = [0]

    def start(source, target, other):
        event = count[0]
        count[0] += 1
        copy = pltpu.make_async_remote_copy(
            source, target, send.at[event], recv.at[event], device_id=other, device_id_type=MESH
        )
        copy.start()
        sent[event] = copy
        return event

    event = start(norm.at[1 - core], piece.at[core], sibling)
    piece[core] = norm[core]
    pltpu.make_async_remote_copy(
        norm.at[core], piece.at[1 - core], send.at[event], recv.at[event], device_id=sibling, device_id_type=MESH
    ).wait_recv()
    both = [piece[s].astype(jnp.float32) for s in (0, 1)]
    for j in (0, 1):
        rows = [both[s][8 * h + 4 * j : 8 * h + 4 * j + 4] for h in (0, 1) for s in (0, 1)]
        units[me[0], me[1], me[2], core, :, j * wide : (j + 1) * wide] = jnp.concatenate(rows, axis=0).astype(jnp.bfloat16)

    def view(part, at, of, span):
        order = ORDERS[part]
        index = [None] * 3
        for axis, value in zip(order, at):
            index[axis] = pl.ds(0, 4) if value is None else value
        first, last, middle = PARTS[part]
        low, high = {0: (first, middle), 1: (middle, last), 2: (first, last)}[span]
        return units.at[index[0], index[1], index[2], of, :, pl.ds(low * TILE, (high - low) * TILE)]

    class Route:
        def __init__(self, part):
            self.part = part
            order = ORDERS[part]
            self.at = [me[axis] for axis in order]
            self.near = {(k, s): device(moved(me, order[k], s), core) for k in range(3) for s in (1, -1, 2)}
            self.events = {}

        def where(self, da, db, dc):
            a, b, c = self.at
            return (None if da is None else (a + da + 4) % 4, (b + db + 4) % 4, (c + dc + 4) % 4)

        def push(self, name, k, step, where, span=2):
            ref = view(self.part, self.where(*where), core, span)
            self.events[name] = start(ref, ref, self.near[k, step])

        def share(self, db, dc):
            ref = view(self.part, self.where(None, db, dc), core, 2)
            self.events["share", db, dc] = start(ref, ref, sibling)

        def arrived(self, name, where, span=2, of=core):
            ref = view(self.part, self.where(*where), of, span)
            event = self.events[name]
            pltpu.make_async_remote_copy(
                ref, ref, send.at[event], recv.at[event], device_id=sibling, device_id_type=MESH
            ).wait_recv()

    routes = [Route(part) for part in range(3)]
    for r in routes:
        for s in (1, -1, 2):
            r.push(("a", s), 0, s, (0, 0, 0))
    for k, name in ((1, "b"), (2, "c")):
        for r in routes:
            for s in (1, -1):
                r.push((name, 0, s, 0), k, s, (0, 0, 0))
    acc[...] = jnp.zeros_like(acc)
    for r in routes:
        for s in (1, -1, 2):
            r.arrived(("a", s), (-s, 0, 0))
        for da in (1, -1, 2):
            for s in (1, -1):
                r.push(("b", 0, s, da), 1, s, (da, 0, 0))
    for r in routes:
        r.share(0, 0)
        for da in (1, -1, 2):
            for s in (1, -1):
                r.push(("c", 0, s, da), 2, s, (da, 0, 0))
    for r in routes:
        for s, span in ((1, 0), (-1, 1)):
            for da in (0, 1, -1, 2):
                r.arrived(("b", 0, s, da), (da, -s, 0))
            r.push(("bb", s), 1, s, (None, -s, 0), span)
    for db in (-1, 1):
        for r in routes:
            for s in (1, -1):
                r.push(("c", db, s), 2, s, (None, db, 0))
            r.share(db, 0)
    for r in routes:
        for s, span in ((1, 0), (-1, 1)):
            r.arrived(("bb", s), (None, 2, 0), span)
        for s in (1, -1):
            r.push(("c", 2, s), 2, s, (None, 2, 0))
        r.share(2, 0)

    def onward(db):
        for r in routes:
            for s, span in ((1, 0), (-1, 1)):
                if db == 0:
                    for da in (0, 1, -1, 2):
                        r.arrived(("c", db, s, da), (da, db, -s))
                else:
                    r.arrived(("c", db, s), (None, db, -s))
                r.push(("cc", db, s), 2, s, (None, db, -s), span)
            for s in (1, -1):
                r.share(db, -s)

    def last(db):
        for r in routes:
            for s, span in ((1, 0), (-1, 1)):
                r.arrived(("cc", db, s), (None, db, 2), span)
            r.share(db, 2)

    def multiply(part, *planes):
        r = routes[part]
        axis = ORDERS[part][2]
        at = [r.where(0, 0, dc)[2] for dc in planes]
        for dc in planes:
            for db in (0, -1, 1, 2):
                r.arrived(("share", db, dc), (None, db, dc), of=1 - core)
        low, high, _ = PARTS[part]
        columns = pl.ds(low * TILE, (high - low) * TILE)
        for of in (0, 1):
            for h in (0, 1):
                rows = []
                for p in at:
                    index = [slice(None)] * 3
                    index[axis] = p
                    rows.append(units[(*index, of, slice(8 * h, 8 * h + 8), columns)].reshape(128, (high - low) * TILE))
                product = jnp.dot(
                    jnp.concatenate(rows, axis=0) if len(rows) > 1 else rows[0],
                    head[of * 2 + h, columns],
                    preferred_element_type=jnp.float32,
                )
                for n, p in enumerate(at):
                    index = [slice(None)] * 3
                    index[axis] = p
                    acc[tuple(index)] += product[n * 128 : (n + 1) * 128].reshape(4, 4, 8, V)

    grp, tp = lax.axis_index("grp"), lax.axis_index("tp")
    here = grp * 8 + tp

    def deliver(at, s, arrival):
        pltpu.make_async_remote_copy(
            codes.at[place(at), s], got.at[here], spread.at[0], spread.at[arrival],
            device_id=device(at, s), device_id_type=MESH,
        ).start()

    def chip(dx, dy, dz):
        return tuple(lax.rem(axis + d, 4) for axis, d in zip(me, (dx, dy, dz)))

    def code(rows, slots):
        anchor = decode(encode(rows[:, :, :1]))
        lane = lax.broadcasted_iota(jnp.int32, rows.shape, 2)
        coded = encode(jnp.where(lane == 0, rows, rows - anchor))
        for s in range(2):
            tiles = [coded[:, 4 * s : 4 * s + 4, TILE * j : TILE * (j + 1)] for j in range(4)]
            message = jnp.concatenate(tiles, axis=1).astype(jnp.bfloat16)
            for n, slot in enumerate(slots):
                codes[slot, s] = message[n]

    def place(at):
        return (at[0] * 4 + at[1]) * 4 + at[2]

    def code_some(chips):
        code(jnp.stack([acc[at] for at in chips]), [place(at) for at in chips])

    def emit(at, arrival=2):
        for s in range(2):
            deliver(at, s, arrival)

    def close(k):
        return lax.rem(k + 3, 4)

    for copy in heads:
        copy.wait()
    onward(0)
    multiply(0, 0)
    onward(-1)
    multiply(1, 0)
    onward(1)
    multiply(2, 0)
    onward(2)
    multiply(0, -1, 1)
    last(0)
    multiply(1, -1, 1)
    last(-1)
    multiply(2, -1, 1)
    last(1)

    def near(k, _):
        for dx in (3, 0, 1):
            code_some([chip(dx, close(k), dz) for dz in (3, 0, 1)])
        for dx in (3, 0, 1):
            for dz in (3, 0, 1):
                if (dx, dz) != (0, 0):
                    emit(chip(dx, close(k), dz), 1)
        return 0

    lax.fori_loop(0, 3, near, 0)
    emit(chip(0, 3, 0), 1)
    emit(chip(0, 1, 0), 1)
    deliver(me, 1 - core, 1)
    got[here] = codes[place(me), core]

    last(2)
    multiply(0, 2)

    def code_and_emit(*sets):
        for chips in sets:
            code_some(chips)
        for chips in sets:
            for at in chips:
                emit(at)

    def z_only(k, _):
        code_and_emit([chip(close(k), dy, 2) for dy in (3, 0, 1)])
        return 0

    lax.fori_loop(0, 3, z_only, 0)
    multiply(1, 2)

    def x_not_y(k, _):
        code_and_emit([chip(2, close(k), dz) for dz in (3, 0, 1, 2)])
        return 0

    lax.fori_loop(0, 3, x_not_y, 0)
    multiply(2, 2)

    def y_all(k, _):
        code_and_emit([chip(2 * k + dx, 2, dz) for dx in (0, 1) for dz in range(4)])
        return 0

    lax.fori_loop(0, 2, y_all, 0)

    def landed(messages, arrival):
        some = got.at[pl.ds(0, messages)]
        return pltpu.make_async_remote_copy(
            some, some, spread.at[0], spread.at[arrival], device_id=sibling, device_id_type=MESH
        )

    def four(rows):
        return jnp.concatenate([rows] * 4, axis=rows.ndim - 2)

    some = 16

    def open_messages(top, chips):
        slots = []
        for at in chips:
            for s in range(2):
                g, t = device(at, s)
                slots.append(g * 8 + t)
        d = decode(jnp.stack([got[slot] for slot in slots]).astype(jnp.float32))
        first = lax.broadcasted_iota(jnp.int32, d.shape, 2) == 0
        first = first & (lax.broadcasted_iota(jnp.int32, d.shape, 1) < 4)
        values = jnp.where(first, d, d + four(d[:, :4, :1]))
        for n, slot in enumerate(slots):
            logits[slot] = values[n]
        return jnp.maximum(top, jnp.max(values, axis=0))

    def open_near(k, top):
        return open_messages(top, [chip(dx, close(k), dz) for dx in (3, 0, 1) for dz in (3, 0, 1)])

    def open_z(k, top):
        return open_messages(top, [chip(close(k), dy, 2) for dy in (3, 0, 1)])

    def open_x(k, top):
        return open_messages(top, [chip(2, close(k), dz) for dz in (3, 0, 1, 2)])

    def open_y(k, top):
        return open_messages(top, [chip(2 * k + dx, 2, dz) for dx in (0, 1) for dz in range(4)])

    def by_token(rows, combine, reduce):
        each = reduce(rows, axis=1, keepdims=True)
        return combine(combine(each[:4], each[4:8]), combine(each[8:12], each[12:]))

    landed(53, 1).wait_recv()
    top = lax.fori_loop(0, 3, open_near, jnp.full((16, TILE), -jnp.inf, jnp.float32))
    landed(74, 2).wait_recv()
    top = lax.fori_loop(0, 3, open_z, top)
    top = lax.fori_loop(0, 3, open_x, top)
    top = lax.fori_loop(0, 2, open_y, top)
    top = by_token(top, jnp.maximum, jnp.max)
    top_rows = jnp.broadcast_to(four(top), (16, TILE))

    def add(n, total):
        return total + jnp.sum(jnp.exp(logits[pl.ds(n * some, some)] - top_rows), axis=0)

    total = lax.fori_loop(0, 128 // some, add, jnp.zeros((16, TILE), jnp.float32))
    total = by_token(total, jnp.add, jnp.sum)
    top_row = jnp.broadcast_to(top, (TOK, TILE))
    log_row = jnp.broadcast_to(jnp.log(total), (TOK, TILE))

    def finish(n, _):
        at = pl.ds(n * some, some)
        for j in range(4):
            out_ref[at, :, TILE * j : TILE * (j + 1)] = logits[at, 4 * j : 4 * j + 4] - top_row - log_row
        return 0

    lax.fori_loop(0, 128 // some, finish, 0)
    landed(127, 1).wait_send()
    for copy in sent.values():
        copy.wait_send()


def on_device(hidden, gain, head):
    log_probs = pl.pallas_call(
        kernel,
        out_shape=jax.ShapeDtypeStruct((128, TOK, V), jnp.float32),
        in_specs=[
            pl.BlockSpec(memory_space=pltpu.HBM),
            pl.BlockSpec(memory_space=pltpu.HBM),
            pl.BlockSpec(memory_space=pltpu.HBM),
        ],
        out_specs=pl.BlockSpec(memory_space=pltpu.VMEM),
        scratch_shapes=[
            pltpu.VMEM((TOK, D), jnp.bfloat16),
            pltpu.VMEM((1, D), jnp.float32),
            pltpu.VMEM((2, 16, D // 8), jnp.bfloat16),
            pltpu.VMEM((2, 16, D // 8), jnp.bfloat16),
            pltpu.VMEM((4, 4, 4, 2, 16, QUARTER), jnp.bfloat16),
            pltpu.VMEM((4, QUARTER, V), jnp.bfloat16),
            pltpu.VMEM((4, 4, 4, 8, V), jnp.float32),
            pltpu.VMEM((64, 2, 16, TILE), jnp.bfloat16),
            pltpu.VMEM((128, 16, TILE), jnp.bfloat16),
            pltpu.VMEM((128, 16, TILE), jnp.float32),
            pltpu.SemaphoreType.DMA((EVENTS,)),
            pltpu.SemaphoreType.DMA((EVENTS,)),
            pltpu.SemaphoreType.DMA((6,)),
            pltpu.SemaphoreType.DMA((3,)),
        ],
        compiler_params=pltpu.CompilerParams(
            collective_id=0, has_side_effects=True, vmem_limit_bytes=50 * 2**20
        ),
        cost_estimate=pl.CostEstimate(
            flops=2 * 512 * D * V, bytes_accessed=D * V * 2, transcendentals=0
        ),
    )(*(pltpu.with_memory_space_constraint(a, pltpu.HBM) for a in (hidden, gain.reshape(1, D), head)))
    return log_probs.transpose(1, 0, 2).reshape(TOK, 128 * V)


def solution(mesh):
    return jax.shard_map(
        on_device,
        mesh=mesh,
        in_specs=(P(("grp", "tp"), None), P(), P(None, ("grp", "tp"))),
        out_specs=P(("grp", "tp"), None),
        check_vma=False,
    )
```

```python
import jax
import jax.numpy as jnp
from jax import lax
from jax.experimental import pallas as pl
from jax.experimental.pallas import tpu as pltpu
from jax.sharding import PartitionSpec as P

MESH = pl.DeviceIdType.MESH
D, V, TOK = 16384, 512, 4
QUARTER = D // 4
TILE = 128
PARTS = ((0, 11, 6), (11, 22, 17), (22, 32, 27))
ORDERS = ((0, 1, 2), (1, 2, 0), (2, 0, 1))
STEEP, FLOOR, LOWEST = 17.5, 8.0, 125.0
EVENTS = 1 + 3 * 51


def position():
    grp, tp = lax.axis_index("grp"), lax.axis_index("tp")
    return (tp // 2, (tp % 2) * 2 + (grp // 2) % 2, grp // 4), grp % 2


def device(at, core):
    x, y, z = at
    return ((z * 2 + y % 2) * 2 + core, x * 2 + y // 2)


def moved(at, axis, step):
    at = list(at)
    at[axis] = (at[axis] + step + 4) % 4
    return tuple(at)


def encode(d):
    size = jnp.exp2(STEEP * jnp.log2(1.0 + jnp.abs(d) * (1.0 / FLOOR)) - LOWEST)
    return jnp.where(d < 0, -size, size).astype(jnp.bfloat16).astype(jnp.float32)


def decode(v):
    size = FLOOR * (jnp.exp2((jnp.log2(jnp.abs(v)) + LOWEST) * (1.0 / STEEP)) - 1.0)
    return jnp.where(v < 0, -size, size)


def kernel(
    hidden_hbm, gain_hbm, head_ref, out_ref, hidden_ref, gain_ref, norm, piece, units, head, acc, codes, got, logits, send, recv, local, spread
):
    me, core = position()
    sibling = device(me, 1 - core)
    inputs = [
        pltpu.make_async_copy(hidden_hbm, hidden_ref, local.at[4]),
        pltpu.make_async_copy(gain_hbm, gain_ref, local.at[5]),
    ]
    for copy in inputs:
        copy.start()
    heads = []
    for quarter in range(4):
        copy = pltpu.make_async_copy(
            head_ref.at[pl.ds(quarter * QUARTER, QUARTER)], head.at[quarter], local.at[quarter]
        )
        copy.start()
        heads.append(copy)

    barrier = pltpu.get_barrier_semaphore()
    greeted = [device(moved(me, axis, step), core) for axis in range(3) for step in (1, -1, 2)]
    greeted.append(sibling)
    for other in greeted:
        pl.semaphore_signal(barrier, inc=1, device_id=other, device_id_type=MESH)

    for copy in inputs:
        copy.wait()
    values = hidden_ref[...].astype(jnp.float32)
    scale = lax.rsqrt(jnp.mean(values * values, axis=-1, keepdims=True) + 1e-05)
    wide = D // 8
    for half in range(2):
        rows = []
        for j in range(4):
            columns = slice(half * 2 * QUARTER + j * wide, half * 2 * QUARTER + (j + 1) * wide)
            rows.append(hidden_ref[:, columns].astype(jnp.float32) * scale * gain_ref[:, columns])
        norm[half] = jnp.concatenate(rows, axis=0).astype(jnp.bfloat16)
    pl.semaphore_wait(barrier, len(greeted))

    sent = {}
    count = [0]

    def start(source, target, other):
        event = count[0]
        count[0] += 1
        copy = pltpu.make_async_remote_copy(
            source, target, send.at[event], recv.at[event], device_id=other, device_id_type=MESH
        )
        copy.start()
        sent[event] = copy
        return event

    event = start(norm.at[1 - core], piece.at[core], sibling)
    piece[core] = norm[core]
    pltpu.make_async_remote_copy(
        norm.at[core], piece.at[1 - core], send.at[event], recv.at[event], device_id=sibling, device_id_type=MESH
    ).wait_recv()
    both = [piece[s].astype(jnp.float32) for s in (0, 1)]
    for j in (0, 1):
        rows = [both[s][8 * h + 4 * j : 8 * h + 4 * j + 4] for h in (0, 1) for s in (0, 1)]
        units[me[0], me[1], me[2], core, :, j * wide : (j + 1) * wide] = jnp.concatenate(rows, axis=0).astype(jnp.bfloat16)

    def view(part, at, of, span):
        order = ORDERS[part]
        index = [None] * 3
        for axis, value in zip(order, at):
            index[axis] = pl.ds(0, 4) if value is None else value
        first, last, middle = PARTS[part]
        low, high = {0: (first, middle), 1: (middle, last), 2: (first, last)}[span]
        return units.at[index[0], index[1], index[2], of, :, pl.ds(low * TILE, (high - low) * TILE)]

    class Route:
        def __init__(self, part):
            self.part = part
            order = ORDERS[part]
            self.at = [me[axis] for axis in order]
            self.near = {(k, s): device(moved(me, order[k], s), core) for k in range(3) for s in (1, -1, 2)}
            self.events = {}

        def where(self, da, db, dc):
            a, b, c = self.at
            return (None if da is None else (a + da + 4) % 4, (b + db + 4) % 4, (c + dc + 4) % 4)

        def push(self, name, k, step, where, span=2):
            ref = view(self.part, self.where(*where), core, span)
            self.events[name] = start(ref, ref, self.near[k, step])

        def share(self, db, dc):
            ref = view(self.part, self.where(None, db, dc), core, 2)
            self.events["share", db, dc] = start(ref, ref, sibling)

        def arrived(self, name, where, span=2, of=core):
            ref = view(self.part, self.where(*where), of, span)
            event = self.events[name]
            pltpu.make_async_remote_copy(
                ref, ref, send.at[event], recv.at[event], device_id=sibling, device_id_type=MESH
            ).wait_recv()

    routes = [Route(part) for part in range(3)]
    for r in routes:
        for s in (1, -1, 2):
            r.push(("a", s), 0, s, (0, 0, 0))
    for k, name in ((1, "b"), (2, "c")):
        for r in routes:
            for s in (1, -1):
                r.push((name, 0, s, 0), k, s, (0, 0, 0))
    acc[...] = jnp.zeros_like(acc)
    for r in routes:
        for s in (1, -1, 2):
            r.arrived(("a", s), (-s, 0, 0))
        for da in (1, -1, 2):
            for s in (1, -1):
                r.push(("b", 0, s, da), 1, s, (da, 0, 0))
    for r in routes:
        r.share(0, 0)
        for da in (1, -1, 2):
            for s in (1, -1):
                r.push(("c", 0, s, da), 2, s, (da, 0, 0))
    for r in routes:
        for s, span in ((1, 0), (-1, 1)):
            for da in (0, 1, -1, 2):
                r.arrived(("b", 0, s, da), (da, -s, 0))
            r.push(("bb", s), 1, s, (None, -s, 0), span)
    for db in (-1, 1):
        for r in routes:
            for s in (1, -1):
                r.push(("c", db, s), 2, s, (None, db, 0))
            r.share(db, 0)
    for r in routes:
        for s, span in ((1, 0), (-1, 1)):
            r.arrived(("bb", s), (None, 2, 0), span)
        for s in (1, -1):
            r.push(("c", 2, s), 2, s, (None, 2, 0))
        r.share(2, 0)

    def onward(db):
        for r in routes:
            for s, span in ((1, 0), (-1, 1)):
                if db == 0:
                    for da in (0, 1, -1, 2):
                        r.arrived(("c", db, s, da), (da, db, -s))
                else:
                    r.arrived(("c", db, s), (None, db, -s))
                r.push(("cc", db, s), 2, s, (None, db, -s), span)
        for r in routes:
            for s in (1, -1):
                r.share(db, -s)

    def last(db):
        for r in routes:
            for s, span in ((1, 0), (-1, 1)):
                r.arrived(("cc", db, s), (None, db, 2), span)
            r.share(db, 2)

    def multiply(part, *planes):
        r = routes[part]
        axis = ORDERS[part][2]
        at = [r.where(0, 0, dc)[2] for dc in planes]
        for dc in planes:
            for db in (0, -1, 1, 2):
                r.arrived(("share", db, dc), (None, db, dc), of=1 - core)
        low, high, _ = PARTS[part]
        columns = pl.ds(low * TILE, (high - low) * TILE)
        wide = (high - low) * TILE
        quarters = [(of, h) for of in (0, 1) for h in (0, 1)]
        rows = []
        for p in at:
            index = [slice(None)] * 3
            index[axis] = p
            rows.append(
                jnp.concatenate(
                    [
                        units[(*index, of, slice(8 * h, 8 * h + 8), columns)].reshape(128, wide)
                        for of, h in quarters
                    ],
                    axis=1,
                )
            )
        product = jnp.dot(
            jnp.concatenate(rows, axis=0) if len(rows) > 1 else rows[0],
            jnp.concatenate([head[of * 2 + h, columns] for of, h in quarters], axis=0),
            preferred_element_type=jnp.float32,
        )
        for n, p in enumerate(at):
            index = [slice(None)] * 3
            index[axis] = p
            acc[tuple(index)] += product[n * 128 : (n + 1) * 128].reshape(4, 4, 8, V)

    grp, tp = lax.axis_index("grp"), lax.axis_index("tp")
    here = grp * 8 + tp

    def deliver(at, s, arrival):
        pltpu.make_async_remote_copy(
            codes.at[place(at), s], got.at[here], spread.at[0], spread.at[arrival],
            device_id=device(at, s), device_id_type=MESH,
        ).start()

    def chip(dx, dy, dz):
        return tuple(lax.rem(axis + d, 4) for axis, d in zip(me, (dx, dy, dz)))

    def code(rows, slots):
        anchor = decode(encode(rows[:, :, :1]))
        lane = lax.broadcasted_iota(jnp.int32, rows.shape, 2)
        coded = encode(jnp.where(lane == 0, rows, rows - anchor))
        for s in range(2):
            tiles = [coded[:, 4 * s : 4 * s + 4, TILE * j : TILE * (j + 1)] for j in range(4)]
            message = jnp.concatenate(tiles, axis=1).astype(jnp.bfloat16)
            for n, slot in enumerate(slots):
                codes[slot, s] = message[n]

    def place(at):
        return (at[0] * 4 + at[1]) * 4 + at[2]

    def code_some(chips):
        code(jnp.stack([acc[at] for at in chips]), [place(at) for at in chips])

    def emit(at, arrival=2):
        for s in range(2):
            deliver(at, s, arrival)

    def close(k):
        return lax.rem(k + 3, 4)

    for copy in heads:
        copy.wait()
    onward(0)
    multiply(0, 0)
    onward(-1)
    multiply(1, 0)
    onward(1)
    multiply(2, 0)
    onward(2)
    multiply(0, -1, 1)
    last(0)
    multiply(1, -1, 1)
    last(-1)
    multiply(2, -1, 1)
    last(1)

    def near(k, _):
        for dx in (3, 0, 1):
            code_some([chip(dx, close(k), dz) for dz in (3, 0, 1)])
        for dx in (3, 0, 1):
            for dz in (3, 0, 1):
                if (dx, dz) != (0, 0):
                    emit(chip(dx, close(k), dz), 1)
        return 0

    lax.fori_loop(0, 3, near, 0)
    emit(chip(0, 3, 0), 1)
    emit(chip(0, 1, 0), 1)
    deliver(me, 1 - core, 1)
    got[here] = codes[place(me), core]

    last(2)
    multiply(0, 2)

    def code_and_emit(*sets):
        for chips in sets:
            code_some(chips)
        for chips in sets:
            for at in chips:
                emit(at)

    def z_only(k, _):
        code_and_emit([chip(close(k), dy, 2) for dy in (3, 0, 1)])
        return 0

    lax.fori_loop(0, 3, z_only, 0)
    multiply(1, 2)

    def x_not_y(k, _):
        code_and_emit([chip(2, close(k), dz) for dz in (3, 0, 1, 2)])
        return 0

    lax.fori_loop(0, 3, x_not_y, 0)
    multiply(2, 2)

    def y_all(k, _):
        code_and_emit([chip(2 * k + dx, 2, dz) for dx in (0, 1) for dz in range(4)])
        return 0

    lax.fori_loop(0, 2, y_all, 0)

    def landed(messages, arrival):
        some = got.at[pl.ds(0, messages)]
        return pltpu.make_async_remote_copy(
            some, some, spread.at[0], spread.at[arrival], device_id=sibling, device_id_type=MESH
        )

    def four(rows):
        return jnp.concatenate([rows] * 4, axis=rows.ndim - 2)

    some = 16

    def open_messages(carry, chips):
        top, total = carry
        slots = []
        for at in chips:
            for s in range(2):
                g, t = device(at, s)
                slots.append(g * 8 + t)
        d = decode(jnp.stack([got[slot] for slot in slots]).astype(jnp.float32))
        first = lax.broadcasted_iota(jnp.int32, d.shape, 2) == 0
        first = first & (lax.broadcasted_iota(jnp.int32, d.shape, 1) < 4)
        values = jnp.where(first, d, d + four(d[:, :4, :1]))
        for n, slot in enumerate(slots):
            logits[slot] = values[n]
        higher = jnp.maximum(top, jnp.max(values, axis=0))
        return higher, total * jnp.exp(top - higher) + jnp.sum(jnp.exp(values - higher), axis=0)

    def open_near(k, carry):
        return open_messages(carry, [chip(dx, close(k), dz) for dx in (3, 0, 1) for dz in (3, 0, 1)])

    def open_z(k, carry):
        return open_messages(carry, [chip(close(k), dy, 2) for dy in (3, 0, 1)])

    def open_x(k, carry):
        return open_messages(carry, [chip(2, close(k), dz) for dz in (3, 0, 1, 2)])

    def open_y(k, carry):
        return open_messages(carry, [chip(2 * k + dx, 2, dz) for dx in (0, 1) for dz in range(4)])

    def by_token(rows, combine, reduce):
        each = reduce(rows, axis=1, keepdims=True)
        return combine(combine(each[:4], each[4:8]), combine(each[8:12], each[12:]))

    carry = (jnp.full((16, TILE), -jnp.inf, jnp.float32), jnp.zeros((16, TILE), jnp.float32))
    landed(53, 1).wait_recv()
    carry = lax.fori_loop(0, 3, open_near, carry)
    landed(74, 2).wait_recv()
    carry = lax.fori_loop(0, 3, open_z, carry)
    carry = lax.fori_loop(0, 3, open_x, carry)
    tops, totals = lax.fori_loop(0, 2, open_y, carry)
    top = jnp.broadcast_to(four(by_token(tops, jnp.maximum, jnp.max)), (16, TILE))
    total = by_token(totals * jnp.exp(tops - top), jnp.add, jnp.sum)
    log_total = jnp.broadcast_to(four(jnp.log(total)), (16, TILE))

    def finish(n, _):
        at = pl.ds(n * some, some)
        out_ref[at] = logits[at] - top - log_total
        return 0

    lax.fori_loop(0, 128 // some, finish, 0)
    landed(127, 1).wait_send()
    for copy in sent.values():
        copy.wait_send()


def on_device(hidden, gain, head):
    log_probs = pl.pallas_call(
        kernel,
        out_shape=jax.ShapeDtypeStruct((128, 16, TILE), jnp.float32),
        in_specs=[
            pl.BlockSpec(memory_space=pltpu.HBM),
            pl.BlockSpec(memory_space=pltpu.HBM),
            pl.BlockSpec(memory_space=pltpu.HBM),
        ],
        out_specs=pl.BlockSpec(memory_space=pltpu.VMEM),
        scratch_shapes=[
            pltpu.VMEM((TOK, D), jnp.bfloat16),
            pltpu.VMEM((1, D), jnp.float32),
            pltpu.VMEM((2, 16, D // 8), jnp.bfloat16),
            pltpu.VMEM((2, 16, D // 8), jnp.bfloat16),
            pltpu.VMEM((4, 4, 4, 2, 16, QUARTER), jnp.bfloat16),
            pltpu.VMEM((4, QUARTER, V), jnp.bfloat16),
            pltpu.VMEM((4, 4, 4, 8, V), jnp.float32),
            pltpu.VMEM((64, 2, 16, TILE), jnp.bfloat16),
            pltpu.VMEM((128, 16, TILE), jnp.bfloat16),
            pltpu.VMEM((128, 16, TILE), jnp.float32),
            pltpu.SemaphoreType.DMA((EVENTS,)),
            pltpu.SemaphoreType.DMA((EVENTS,)),
            pltpu.SemaphoreType.DMA((6,)),
            pltpu.SemaphoreType.DMA((3,)),
        ],
        compiler_params=pltpu.CompilerParams(
            collective_id=0, has_side_effects=True, vmem_limit_bytes=50 * 2**20
        ),
        cost_estimate=pl.CostEstimate(
            flops=2 * 512 * D * V, bytes_accessed=D * V * 2, transcendentals=0
        ),
    )(*(pltpu.with_memory_space_constraint(a, pltpu.HBM) for a in (hidden, gain.reshape(1, D), head)))
    return log_probs.reshape(128 * 4, TOK, TILE).transpose(1, 0, 2).reshape(TOK, 128 * V)


def solution(mesh):
    return jax.shard_map(
        on_device,
        mesh=mesh,
        in_specs=(P(("grp", "tp"), None), P(), P(None, ("grp", "tp"))),
        out_specs=P(("grp", "tp"), None),
        check_vma=False,
    )
```

```python
import jax
import jax.numpy as jnp
from jax import lax
from jax.experimental import pallas as pl
from jax.experimental.pallas import tpu as pltpu
from jax.sharding import PartitionSpec as P

MESH = pl.DeviceIdType.MESH
D, V, TOK = 16384, 512, 4
QUARTER = D // 4
TILE = 128
PARTS = ((0, 11, 6), (11, 22, 17), (22, 32, 27))
ORDERS = ((0, 1, 2), (1, 2, 0), (2, 0, 1))
STEEP, FLOOR, LOWEST = 17.5, 8.0, 125.0
EVENTS = 1 + 3 * 51


def position():
    grp, tp = lax.axis_index("grp"), lax.axis_index("tp")
    return (tp // 2, (tp % 2) * 2 + (grp // 2) % 2, grp // 4), grp % 2


def device(at, core):
    x, y, z = at
    return ((z * 2 + y % 2) * 2 + core, x * 2 + y // 2)


def moved(at, axis, step):
    at = list(at)
    at[axis] = (at[axis] + step + 4) % 4
    return tuple(at)


def encode(d):
    size = jnp.exp2(STEEP * jnp.log2(1.0 + jnp.abs(d) * (1.0 / FLOOR)) - LOWEST)
    return jnp.where(d < 0, -size, size).astype(jnp.bfloat16).astype(jnp.float32)


def decode(v):
    size = FLOOR * (jnp.exp2((jnp.log2(jnp.abs(v)) + LOWEST) * (1.0 / STEEP)) - 1.0)
    return jnp.where(v < 0, -size, size)


def kernel(
    hidden_hbm, gain_hbm, head_ref, out_ref, hidden_ref, gain_ref, norm, piece, units, head, acc, codes, got, logits, send, recv, local, spread
):
    me, core = position()
    sibling = device(me, 1 - core)
    inputs = [
        pltpu.make_async_copy(hidden_hbm, hidden_ref, local.at[4]),
        pltpu.make_async_copy(gain_hbm, gain_ref, local.at[5]),
    ]
    for copy in inputs:
        copy.start()
    heads = []
    for quarter in range(4):
        copy = pltpu.make_async_copy(
            head_ref.at[pl.ds(quarter * QUARTER, QUARTER)], head.at[quarter], local.at[quarter]
        )
        copy.start()
        heads.append(copy)

    barrier = pltpu.get_barrier_semaphore()
    greeted = [device(moved(me, axis, step), core) for axis in range(3) for step in (1, -1, 2)]
    greeted.append(sibling)
    for other in greeted:
        pl.semaphore_signal(barrier, inc=1, device_id=other, device_id_type=MESH)

    for copy in inputs:
        copy.wait()
    values = hidden_ref[...].astype(jnp.float32)
    scale = lax.rsqrt(jnp.mean(values * values, axis=-1, keepdims=True) + 1e-05)
    wide = D // 8
    for half in range(2):
        rows = []
        for j in range(4):
            columns = slice(half * 2 * QUARTER + j * wide, half * 2 * QUARTER + (j + 1) * wide)
            rows.append(hidden_ref[:, columns].astype(jnp.float32) * scale * gain_ref[:, columns])
        norm[half] = jnp.concatenate(rows, axis=0).astype(jnp.bfloat16)
    pl.semaphore_wait(barrier, len(greeted))

    sent = {}
    count = [0]

    def start(source, target, other):
        event = count[0]
        count[0] += 1
        copy = pltpu.make_async_remote_copy(
            source, target, send.at[event], recv.at[event], device_id=other, device_id_type=MESH
        )
        copy.start()
        sent[event] = copy
        return event

    event = start(norm.at[1 - core], piece.at[core], sibling)
    piece[core] = norm[core]
    pltpu.make_async_remote_copy(
        norm.at[core], piece.at[1 - core], send.at[event], recv.at[event], device_id=sibling, device_id_type=MESH
    ).wait_recv()
    both = [piece[s].astype(jnp.float32) for s in (0, 1)]
    for j in (0, 1):
        rows = [both[s][8 * h + 4 * j : 8 * h + 4 * j + 4] for h in (0, 1) for s in (0, 1)]
        units[me[0], me[1], me[2], core, :, j * wide : (j + 1) * wide] = jnp.concatenate(rows, axis=0).astype(jnp.bfloat16)

    def view(part, at, of, span):
        order = ORDERS[part]
        index = [None] * 3
        for axis, value in zip(order, at):
            index[axis] = pl.ds(0, 4) if value is None else value
        first, last, middle = PARTS[part]
        low, high = {0: (first, middle), 1: (middle, last), 2: (first, last)}[span]
        return units.at[index[0], index[1], index[2], of, :, pl.ds(low * TILE, (high - low) * TILE)]

    class Route:
        def __init__(self, part):
            self.part = part
            order = ORDERS[part]
            self.at = [me[axis] for axis in order]
            self.near = {(k, s): device(moved(me, order[k], s), core) for k in range(3) for s in (1, -1, 2)}
            self.events = {}

        def where(self, da, db, dc):
            a, b, c = self.at
            return (None if da is None else (a + da + 4) % 4, (b + db + 4) % 4, (c + dc + 4) % 4)

        def push(self, name, k, step, where, span=2):
            ref = view(self.part, self.where(*where), core, span)
            self.events[name] = start(ref, ref, self.near[k, step])

        def share(self, db, dc):
            ref = view(self.part, self.where(None, db, dc), core, 2)
            self.events["share", db, dc] = start(ref, ref, sibling)

        def arrived(self, name, where, span=2, of=core):
            ref = view(self.part, self.where(*where), of, span)
            event = self.events[name]
            pltpu.make_async_remote_copy(
                ref, ref, send.at[event], recv.at[event], device_id=sibling, device_id_type=MESH
            ).wait_recv()

    routes = [Route(part) for part in range(3)]
    for r in routes:
        for s in (1, -1, 2):
            r.push(("a", s), 0, s, (0, 0, 0))
    for k, name in ((1, "b"), (2, "c")):
        for r in routes:
            for s in (1, -1):
                r.push((name, 0, s, 0), k, s, (0, 0, 0))
    acc[...] = jnp.zeros_like(acc)
    for r in routes:
        for s in (1, -1, 2):
            r.arrived(("a", s), (-s, 0, 0))
        for da in (1, -1, 2):
            for s in (1, -1):
                r.push(("b", 0, s, da), 1, s, (da, 0, 0))
    for r in routes:
        r.share(0, 0)
        for da in (1, -1, 2):
            for s in (1, -1):
                r.push(("c", 0, s, da), 2, s, (da, 0, 0))
    for r in routes:
        for s, span in ((1, 0), (-1, 1)):
            for da in (0, 1, -1, 2):
                r.arrived(("b", 0, s, da), (da, -s, 0))
            r.push(("bb", s), 1, s, (None, -s, 0), span)
    for db in (-1, 1):
        for r in routes:
            for s in (1, -1):
                r.push(("c", db, s), 2, s, (None, db, 0))
            r.share(db, 0)
    for r in routes:
        for s, span in ((1, 0), (-1, 1)):
            r.arrived(("bb", s), (None, 2, 0), span)
        for s in (1, -1):
            r.push(("c", 2, s), 2, s, (None, 2, 0))
        r.share(2, 0)

    def onward(db):
        for r in routes:
            for s, span in ((1, 0), (-1, 1)):
                if db == 0:
                    for da in (0, 1, -1, 2):
                        r.arrived(("c", db, s, da), (da, db, -s))
                else:
                    r.arrived(("c", db, s), (None, db, -s))
                r.push(("cc", db, s), 2, s, (None, db, -s), span)
        for r in routes:
            for s in (1, -1):
                r.share(db, -s)

    def last(db):
        for r in routes:
            for s, span in ((1, 0), (-1, 1)):
                r.arrived(("cc", db, s), (None, db, 2), span)
            r.share(db, 2)

    def multiply(part, *planes):
        r = routes[part]
        axis = ORDERS[part][2]
        at = [r.where(0, 0, dc)[2] for dc in planes]
        for dc in planes:
            for db in (0, -1, 1, 2):
                r.arrived(("share", db, dc), (None, db, dc), of=1 - core)
        low, high, _ = PARTS[part]
        columns = pl.ds(low * TILE, (high - low) * TILE)
        wide = (high - low) * TILE
        quarters = [(of, h) for of in (0, 1) for h in (0, 1)]
        rows = []
        for p in at:
            index = [slice(None)] * 3
            index[axis] = p
            rows.append(
                jnp.concatenate(
                    [
                        units[(*index, of, slice(8 * h, 8 * h + 8), columns)].reshape(128, wide)
                        for of, h in quarters
                    ],
                    axis=1,
                )
            )
        product = jnp.dot(
            jnp.concatenate(rows, axis=0) if len(rows) > 1 else rows[0],
            jnp.concatenate([head[of * 2 + h, columns] for of, h in quarters], axis=0),
            preferred_element_type=jnp.float32,
        )
        for n, p in enumerate(at):
            index = [slice(None)] * 3
            index[axis] = p
            acc[tuple(index)] += product[n * 128 : (n + 1) * 128].reshape(4, 4, 8, V)

    grp, tp = lax.axis_index("grp"), lax.axis_index("tp")
    here = grp * 8 + tp

    def deliver(at, s, arrival):
        pltpu.make_async_remote_copy(
            codes.at[place(at), s], got.at[here], spread.at[0], spread.at[arrival],
            device_id=device(at, s), device_id_type=MESH,
        ).start()

    def chip(dx, dy, dz):
        return tuple(lax.rem(axis + d, 4) for axis, d in zip(me, (dx, dy, dz)))

    def code(rows, slots):
        anchor = decode(encode(rows[:, :, :1]))
        lane = lax.broadcasted_iota(jnp.int32, rows.shape, 2)
        coded = encode(jnp.where(lane == 0, rows, rows - anchor))
        for s in range(2):
            tiles = [coded[:, 4 * s : 4 * s + 4, TILE * j : TILE * (j + 1)] for j in range(4)]
            message = jnp.concatenate(tiles, axis=1).astype(jnp.bfloat16)
            for n, slot in enumerate(slots):
                codes[slot, s] = message[n]

    def place(at):
        return (at[0] * 4 + at[1]) * 4 + at[2]

    def code_some(chips):
        code(jnp.stack([acc[at] for at in chips]), [place(at) for at in chips])

    def emit(at, arrival=2):
        for s in range(2):
            deliver(at, s, arrival)

    def close(k):
        return lax.rem(k + 3, 4)

    for copy in heads:
        copy.wait()
    onward(0)
    multiply(0, 0)
    onward(-1)
    multiply(1, 0)
    onward(1)
    multiply(2, 0)
    onward(2)
    multiply(0, -1, 1)
    last(0)
    multiply(1, -1, 1)
    last(-1)
    multiply(2, -1, 1)
    last(1)

    near_by = (3, 0, 1)
    near = [[chip(dx, dy, dz) for dx in near_by for dz in near_by] for dy in near_by]
    for n, chips in enumerate(near):
        code_some(chips)
        for at in chips:
            if n != 1 or at is not chips[4]:
                emit(at, 1)
    deliver(me, 1 - core, 1)
    got[here] = codes[place(me), core]

    last(2)
    multiply(0, 2)

    def code_and_emit(*sets):
        for chips in sets:
            code_some(chips)
        for chips in sets:
            for at in chips:
                emit(at)

    z_only = [chip(dx, dy, 2) for dx in near_by for dy in near_by]
    x_not_y = [chip(2, dy, dz) for dy in near_by for dz in (*near_by, 2)]
    y_all = [chip(dx, 2, dz) for dx in (2, *near_by) for dz in (2, *near_by)]
    code_and_emit(z_only)
    multiply(1, 2)

    code_and_emit(x_not_y)
    multiply(2, 2)

    code_and_emit(y_all[:8], y_all[8:])

    def landed(messages, arrival):
        some = got.at[pl.ds(0, messages)]
        return pltpu.make_async_remote_copy(
            some, some, spread.at[0], spread.at[arrival], device_id=sibling, device_id_type=MESH
        )

    def four(rows):
        return jnp.concatenate([rows] * 4, axis=rows.ndim - 2)

    some = 16

    def open_messages(carry, chips):
        top, total = carry
        slots = []
        for at in chips:
            for s in range(2):
                g, t = device(at, s)
                slots.append(g * 8 + t)
        d = decode(jnp.stack([got[slot] for slot in slots]).astype(jnp.float32))
        first = lax.broadcasted_iota(jnp.int32, d.shape, 2) == 0
        first = first & (lax.broadcasted_iota(jnp.int32, d.shape, 1) < 4)
        values = jnp.where(first, d, d + four(d[:, :4, :1]))
        for n, slot in enumerate(slots):
            logits[slot] = values[n]
        higher = jnp.maximum(top, jnp.max(values, axis=0))
        return higher, total * jnp.exp(top - higher) + jnp.sum(jnp.exp(values - higher), axis=0)

    def by_token(rows, combine, reduce):
        each = reduce(rows, axis=1, keepdims=True)
        return combine(combine(each[:4], each[4:8]), combine(each[8:12], each[12:]))

    carry = (jnp.full((16, TILE), -jnp.inf, jnp.float32), jnp.zeros((16, TILE), jnp.float32))
    landed(53, 1).wait_recv()
    for chips in near:
        carry = open_messages(carry, chips)
    landed(74, 2).wait_recv()
    for chips in (z_only, x_not_y[:6], x_not_y[6:], y_all[:8], y_all[8:]):
        carry = open_messages(carry, chips)
    tops, totals = carry
    top = jnp.broadcast_to(four(by_token(tops, jnp.maximum, jnp.max)), (16, TILE))
    total = by_token(totals * jnp.exp(tops - top), jnp.add, jnp.sum)
    log_total = jnp.broadcast_to(four(jnp.log(total)), (16, TILE))

    def finish(n, _):
        at = pl.ds(n * some, some)
        out_ref[at] = logits[at] - top - log_total
        return 0

    lax.fori_loop(0, 128 // some, finish, 0, unroll=2)
    landed(127, 1).wait_send()
    for copy in sent.values():
        copy.wait_send()


def on_device(hidden, gain, head):
    log_probs = pl.pallas_call(
        kernel,
        out_shape=jax.ShapeDtypeStruct((128, 16, TILE), jnp.float32),
        in_specs=[
            pl.BlockSpec(memory_space=pltpu.HBM),
            pl.BlockSpec(memory_space=pltpu.HBM),
            pl.BlockSpec(memory_space=pltpu.HBM),
        ],
        out_specs=pl.BlockSpec(memory_space=pltpu.VMEM),
        scratch_shapes=[
            pltpu.VMEM((TOK, D), jnp.bfloat16),
            pltpu.VMEM((1, D), jnp.float32),
            pltpu.VMEM((2, 16, D // 8), jnp.bfloat16),
            pltpu.VMEM((2, 16, D // 8), jnp.bfloat16),
            pltpu.VMEM((4, 4, 4, 2, 16, QUARTER), jnp.bfloat16),
            pltpu.VMEM((4, QUARTER, V), jnp.bfloat16),
            pltpu.VMEM((4, 4, 4, 8, V), jnp.float32),
            pltpu.VMEM((64, 2, 16, TILE), jnp.bfloat16),
            pltpu.VMEM((128, 16, TILE), jnp.bfloat16),
            pltpu.VMEM((128, 16, TILE), jnp.float32),
            pltpu.SemaphoreType.DMA((EVENTS,)),
            pltpu.SemaphoreType.DMA((EVENTS,)),
            pltpu.SemaphoreType.DMA((6,)),
            pltpu.SemaphoreType.DMA((3,)),
        ],
        compiler_params=pltpu.CompilerParams(
            collective_id=0, has_side_effects=True, vmem_limit_bytes=50 * 2**20
        ),
        cost_estimate=pl.CostEstimate(
            flops=2 * 512 * D * V, bytes_accessed=D * V * 2, transcendentals=0
        ),
    )(*(pltpu.with_memory_space_constraint(a, pltpu.HBM) for a in (hidden, gain.reshape(1, D), head)))
    return log_probs.reshape(128 * 4, TOK, TILE).transpose(1, 0, 2).reshape(TOK, 128 * V)


def solution(mesh):
    return jax.shard_map(
        on_device,
        mesh=mesh,
        in_specs=(P(("grp", "tp"), None), P(), P(None, ("grp", "tp"))),
        out_specs=P(("grp", "tp"), None),
        check_vma=False,
    )
```

```python
import jax
import jax.numpy as jnp
from jax import lax
from jax.experimental import pallas as pl
from jax.experimental.pallas import tpu as pltpu
from jax.sharding import PartitionSpec as P

MESH = pl.DeviceIdType.MESH
D, V, TOK = 16384, 512, 4
QUARTER = D // 4
TILE = 128
PARTS = ((0, 11, 6), (11, 22, 17), (22, 32, 27))
ORDERS = ((0, 1, 2), (1, 2, 0), (2, 0, 1))
STEEP, FLOOR, LOWEST = 17.5, 8.0, 125.0
EVENTS = 1 + 3 * 51


def position():
    grp, tp = lax.axis_index("grp"), lax.axis_index("tp")
    return (tp // 2, (tp % 2) * 2 + (grp // 2) % 2, grp // 4), grp % 2


def device(at, core):
    x, y, z = at
    return ((z * 2 + y % 2) * 2 + core, x * 2 + y // 2)


def moved(at, axis, step):
    at = list(at)
    at[axis] = (at[axis] + step + 4) % 4
    return tuple(at)


def encode(d):
    size = jnp.exp2(STEEP * jnp.log2(1.0 + jnp.abs(d) * (1.0 / FLOOR)) - LOWEST)
    return jnp.where(d < 0, -size, size).astype(jnp.bfloat16).astype(jnp.float32)


def decode(v):
    size = FLOOR * (jnp.exp2((jnp.log2(jnp.abs(v)) + LOWEST) * (1.0 / STEEP)) - 1.0)
    return jnp.where(v < 0, -size, size)


def kernel(
    hidden_hbm, gain_hbm, head_ref, out_ref, hidden_ref, gain_ref, norm, piece, units, head, acc, codes, got, logits, send, recv, local, spread
):
    me, core = position()
    sibling = device(me, 1 - core)
    inputs = [
        pltpu.make_async_copy(hidden_hbm, hidden_ref, local.at[4]),
        pltpu.make_async_copy(gain_hbm, gain_ref, local.at[5]),
    ]
    for copy in inputs:
        copy.start()
    heads = []
    for quarter in range(4):
        copy = pltpu.make_async_copy(
            head_ref.at[pl.ds(quarter * QUARTER, QUARTER)], head.at[quarter], local.at[quarter]
        )
        copy.start()
        heads.append(copy)

    barrier = pltpu.get_barrier_semaphore()
    greeted = [device(moved(me, axis, step), core) for axis in range(3) for step in (1, -1, 2)]
    greeted.append(sibling)
    for other in greeted:
        pl.semaphore_signal(barrier, inc=1, device_id=other, device_id_type=MESH)

    for copy in inputs:
        copy.wait()
    values = hidden_ref[...].astype(jnp.float32)
    scale = lax.rsqrt(jnp.mean(values * values, axis=-1, keepdims=True) + 1e-05)
    wide = D // 8
    for half in range(2):
        rows = []
        for j in range(4):
            columns = slice(half * 2 * QUARTER + j * wide, half * 2 * QUARTER + (j + 1) * wide)
            rows.append(hidden_ref[:, columns].astype(jnp.float32) * scale * gain_ref[:, columns])
        norm[half] = jnp.concatenate(rows, axis=0).astype(jnp.bfloat16)
    pl.semaphore_wait(barrier, len(greeted))

    sent = {}
    count = [0]

    def start(source, target, other):
        event = count[0]
        count[0] += 1
        copy = pltpu.make_async_remote_copy(
            source, target, send.at[event], recv.at[event], device_id=other, device_id_type=MESH
        )
        copy.start()
        sent[event] = copy
        return event

    event = start(norm.at[1 - core], piece.at[core], sibling)
    piece[core] = norm[core]
    pltpu.make_async_remote_copy(
        norm.at[core], piece.at[1 - core], send.at[event], recv.at[event], device_id=sibling, device_id_type=MESH
    ).wait_recv()
    both = [piece[s].astype(jnp.float32) for s in (0, 1)]
    for j in (0, 1):
        rows = [both[s][8 * h + 4 * j : 8 * h + 4 * j + 4] for h in (0, 1) for s in (0, 1)]
        units[me[0], me[1], me[2], core, :, j * wide : (j + 1) * wide] = jnp.concatenate(rows, axis=0).astype(jnp.bfloat16)

    def view(part, at, of, span):
        order = ORDERS[part]
        index = [None] * 3
        for axis, value in zip(order, at):
            index[axis] = pl.ds(0, 4) if value is None else value
        first, last, middle = PARTS[part]
        low, high = {0: (first, middle), 1: (middle, last), 2: (first, last)}[span]
        return units.at[index[0], index[1], index[2], of, :, pl.ds(low * TILE, (high - low) * TILE)]

    class Route:
        def __init__(self, part):
            self.part = part
            order = ORDERS[part]
            self.at = [me[axis] for axis in order]
            self.near = {(k, s): device(moved(me, order[k], s), core) for k in range(3) for s in (1, -1, 2)}
            self.events = {}

        def where(self, da, db, dc):
            a, b, c = self.at
            return (None if da is None else (a + da + 4) % 4, (b + db + 4) % 4, (c + dc + 4) % 4)

        def push(self, name, k, step, where, span=2):
            ref = view(self.part, self.where(*where), core, span)
            self.events[name] = start(ref, ref, self.near[k, step])

        def share(self, db, dc):
            ref = view(self.part, self.where(None, db, dc), core, 2)
            self.events["share", db, dc] = start(ref, ref, sibling)

        def arrived(self, name, where, span=2, of=core):
            ref = view(self.part, self.where(*where), of, span)
            event = self.events[name]
            pltpu.make_async_remote_copy(
                ref, ref, send.at[event], recv.at[event], device_id=sibling, device_id_type=MESH
            ).wait_recv()

    routes = [Route(part) for part in range(3)]
    for r in routes:
        for s in (1, -1, 2):
            r.push(("a", s), 0, s, (0, 0, 0))
    for k, name in ((1, "b"), (2, "c")):
        for r in routes:
            for s in (1, -1):
                r.push((name, 0, s, 0), k, s, (0, 0, 0))
    acc[...] = jnp.zeros_like(acc)
    for r in routes:
        for s in (1, -1, 2):
            r.arrived(("a", s), (-s, 0, 0))
        for da in (1, -1, 2):
            for s in (1, -1):
                r.push(("b", 0, s, da), 1, s, (da, 0, 0))
    for r in routes:
        r.share(0, 0)
        for da in (1, -1, 2):
            for s in (1, -1):
                r.push(("c", 0, s, da), 2, s, (da, 0, 0))
    for r in routes:
        for s, span in ((1, 0), (-1, 1)):
            for da in (0, 1, -1, 2):
                r.arrived(("b", 0, s, da), (da, -s, 0))
            r.push(("bb", s), 1, s, (None, -s, 0), span)
    for db in (-1, 1):
        for r in routes:
            for s in (1, -1):
                r.push(("c", db, s), 2, s, (None, db, 0))
            r.share(db, 0)
    for r in routes:
        for s, span in ((1, 0), (-1, 1)):
            r.arrived(("bb", s), (None, 2, 0), span)
        for s in (1, -1):
            r.push(("c", 2, s), 2, s, (None, 2, 0))
        r.share(2, 0)

    def halves(db):
        return ((1, 0), (-1, 1)) if db in (0, -1) else ((1, 1), (-1, 0))

    def onward(db):
        for r in routes:
            for s, span in halves(db):
                if db == 0:
                    for da in (0, 1, -1, 2):
                        r.arrived(("c", db, s, da), (da, db, -s))
                else:
                    r.arrived(("c", db, s), (None, db, -s))
                r.push(("cc", db, s), 2, s, (None, db, -s), span)
        for r in routes:
            for s in (1, -1):
                r.share(db, -s)

    def last(db):
        for r in routes:
            for s, span in halves(db):
                r.arrived(("cc", db, s), (None, db, 2), span)
            r.share(db, 2)

    def multiply(part, *planes):
        r = routes[part]
        axis = ORDERS[part][2]
        at = [r.where(0, 0, dc)[2] for dc in planes]
        for dc in planes:
            for db in (0, -1, 1, 2):
                r.arrived(("share", db, dc), (None, db, dc), of=1 - core)
        low, high, _ = PARTS[part]
        columns = pl.ds(low * TILE, (high - low) * TILE)
        wide = (high - low) * TILE
        quarters = [(of, h) for of in (0, 1) for h in (0, 1)]
        rows = []
        for p in at:
            index = [slice(None)] * 3
            index[axis] = p
            rows.append(
                jnp.concatenate(
                    [
                        units[(*index, of, slice(8 * h, 8 * h + 8), columns)].reshape(128, wide)
                        for of, h in quarters
                    ],
                    axis=1,
                )
            )
        product = jnp.dot(
            jnp.concatenate(rows, axis=0) if len(rows) > 1 else rows[0],
            jnp.concatenate([head[of * 2 + h, columns] for of, h in quarters], axis=0),
            preferred_element_type=jnp.float32,
        )
        for n, p in enumerate(at):
            index = [slice(None)] * 3
            index[axis] = p
            acc[tuple(index)] += product[n * 128 : (n + 1) * 128].reshape(4, 4, 8, V)

    grp, tp = lax.axis_index("grp"), lax.axis_index("tp")
    here = grp * 8 + tp

    def deliver(at, s, arrival):
        pltpu.make_async_remote_copy(
            codes.at[place(at), s], got.at[here], spread.at[0], spread.at[arrival],
            device_id=device(at, s), device_id_type=MESH,
        ).start()

    def chip(dx, dy, dz):
        return tuple(lax.rem(axis + d, 4) for axis, d in zip(me, (dx, dy, dz)))

    def code(rows, slots):
        anchor = decode(encode(rows[:, :, :1]))
        lane = lax.broadcasted_iota(jnp.int32, rows.shape, 2)
        coded = encode(jnp.where(lane == 0, rows, rows - anchor))
        for s in range(2):
            tiles = [coded[:, 4 * s : 4 * s + 4, TILE * j : TILE * (j + 1)] for j in range(4)]
            message = jnp.concatenate(tiles, axis=1).astype(jnp.bfloat16)
            for n, slot in enumerate(slots):
                codes[slot, s] = message[n]

    def place(at):
        return (at[0] * 4 + at[1]) * 4 + at[2]

    def code_some(chips):
        code(jnp.stack([acc[at] for at in chips]), [place(at) for at in chips])

    def emit(at, arrival=2):
        for s in range(2):
            deliver(at, s, arrival)

    def close(k):
        return lax.rem(k + 3, 4)

    for copy in heads:
        copy.wait()
    onward(0)
    multiply(0, 0)
    onward(-1)
    multiply(1, 0)
    onward(1)
    multiply(2, 0)
    onward(2)
    multiply(0, -1, 1)
    last(0)
    multiply(1, -1, 1)
    last(-1)
    multiply(2, -1, 1)
    last(1)

    near_by = (3, 0, 1)
    near = [[chip(dx, dy, dz) for dx in near_by for dz in near_by] for dy in near_by]
    for n, chips in enumerate(near):
        code_some(chips)
        for at in chips:
            if n != 1 or at is not chips[4]:
                emit(at, 1)
    deliver(me, 1 - core, 1)
    got[here] = codes[place(me), core]

    last(2)
    multiply(0, 2)

    def code_and_emit(*sets):
        for chips in sets:
            code_some(chips)
        for chips in sets:
            for at in chips:
                emit(at)

    z_only = [chip(dx, dy, 2) for dx in near_by for dy in near_by]
    x_not_y = [chip(2, dy, dz) for dy in near_by for dz in (*near_by, 2)]
    y_all = [chip(dx, 2, dz) for dx in (2, *near_by) for dz in (2, *near_by)]
    code_and_emit(z_only)
    multiply(1, 2)

    code_and_emit(x_not_y)
    multiply(2, 2)

    code_and_emit(y_all[:8], y_all[8:])

    def landed(messages, arrival):
        some = got.at[pl.ds(0, messages)]
        return pltpu.make_async_remote_copy(
            some, some, spread.at[0], spread.at[arrival], device_id=sibling, device_id_type=MESH
        )

    def four(rows):
        return jnp.concatenate([rows] * 4, axis=rows.ndim - 2)

    some = 16

    def open_messages(carry, chips):
        top, total = carry
        slots = []
        for at in chips:
            for s in range(2):
                g, t = device(at, s)
                slots.append(g * 8 + t)
        d = decode(jnp.stack([got[slot] for slot in slots]).astype(jnp.float32))
        first = lax.broadcasted_iota(jnp.int32, d.shape, 2) == 0
        first = first & (lax.broadcasted_iota(jnp.int32, d.shape, 1) < 4)
        values = jnp.where(first, d, d + four(d[:, :4, :1]))
        for n, slot in enumerate(slots):
            logits[slot] = values[n]
        higher = jnp.maximum(top, jnp.max(values, axis=0))
        return higher, total * jnp.exp(top - higher) + jnp.sum(jnp.exp(values - higher), axis=0)

    def by_token(rows, combine, reduce):
        each = reduce(rows, axis=1, keepdims=True)
        return combine(combine(each[:4], each[4:8]), combine(each[8:12], each[12:]))

    carry = (jnp.full((16, TILE), -jnp.inf, jnp.float32), jnp.zeros((16, TILE), jnp.float32))
    landed(53, 1).wait_recv()
    for chips in near:
        carry = open_messages(carry, chips)
    landed(74, 2).wait_recv()
    for chips in (z_only, x_not_y[:6], x_not_y[6:], y_all[:8], y_all[8:]):
        carry = open_messages(carry, chips)
    tops, totals = carry
    top = jnp.broadcast_to(four(by_token(tops, jnp.maximum, jnp.max)), (16, TILE))
    total = by_token(totals * jnp.exp(tops - top), jnp.add, jnp.sum)
    log_total = jnp.broadcast_to(four(jnp.log(total)), (16, TILE))

    def finish(n, _):
        at = pl.ds(n * some, some)
        out_ref[at] = logits[at] - top - log_total
        return 0

    lax.fori_loop(0, 128 // some, finish, 0, unroll=2)
    landed(127, 1).wait_send()
    for copy in sent.values():
        copy.wait_send()


def on_device(hidden, gain, head):
    log_probs = pl.pallas_call(
        kernel,
        out_shape=jax.ShapeDtypeStruct((128, 16, TILE), jnp.float32),
        in_specs=[
            pl.BlockSpec(memory_space=pltpu.HBM),
            pl.BlockSpec(memory_space=pltpu.HBM),
            pl.BlockSpec(memory_space=pltpu.HBM),
        ],
        out_specs=pl.BlockSpec(memory_space=pltpu.VMEM),
        scratch_shapes=[
            pltpu.VMEM((TOK, D), jnp.bfloat16),
            pltpu.VMEM((1, D), jnp.float32),
            pltpu.VMEM((2, 16, D // 8), jnp.bfloat16),
            pltpu.VMEM((2, 16, D // 8), jnp.bfloat16),
            pltpu.VMEM((4, 4, 4, 2, 16, QUARTER), jnp.bfloat16),
            pltpu.VMEM((4, QUARTER, V), jnp.bfloat16),
            pltpu.VMEM((4, 4, 4, 8, V), jnp.float32),
            pltpu.VMEM((64, 2, 16, TILE), jnp.bfloat16),
            pltpu.VMEM((128, 16, TILE), jnp.bfloat16),
            pltpu.VMEM((128, 16, TILE), jnp.float32),
            pltpu.SemaphoreType.DMA((EVENTS,)),
            pltpu.SemaphoreType.DMA((EVENTS,)),
            pltpu.SemaphoreType.DMA((6,)),
            pltpu.SemaphoreType.DMA((3,)),
        ],
        compiler_params=pltpu.CompilerParams(
            collective_id=0, has_side_effects=True, vmem_limit_bytes=50 * 2**20
        ),
        cost_estimate=pl.CostEstimate(
            flops=2 * 512 * D * V, bytes_accessed=D * V * 2, transcendentals=0
        ),
    )(*(pltpu.with_memory_space_constraint(a, pltpu.HBM) for a in (hidden, gain.reshape(1, D), head)))
    return log_probs.reshape(128 * 4, TOK, TILE).transpose(1, 0, 2).reshape(TOK, 128 * V)


def solution(mesh):
    return jax.shard_map(
        on_device,
        mesh=mesh,
        in_specs=(P(("grp", "tp"), None), P(), P(None, ("grp", "tp"))),
        out_specs=P(("grp", "tp"), None),
        check_vma=False,
    )
```
